128 devices in a mesh: node: 8 (over x_hi, z), local: 16 (over y, x_lo, core).
Axes of the slice: x: 4 (x_hi: 2, x_lo: 2; x = x_hi * 2 + x_lo), y: 4, z: 4, core: 2. Of those that a mesh axis runs over, the one named last changes fastest.
Arguments:
- hidden_acts: bfloat16 [163840, 1024], P(('node', 'local')), may hold values from -8 to 8
- grad_out: bfloat16 [163840, 8192], P(('node', 'local')), may hold values from -0.0390625 to 0.0390625
Outputs:
- grad_shard: float32 [1024, 8192], P(('node', 'local'))
The draws below stay inside these ranges and needn't reach their ends.
All inputs are finite; a program needn't handle non-finite values.
Results may differ from the reference program's by a relative error of at most 0.0003.
Values may be sent and summed in bfloat16 or wider, within the bound.
A program may use at most 256 MiB of HBM per device.

```python
import jax
import jax.numpy as jnp
from jax import lax

D = 8192
QB = 128
TOK_DEV = 1280
ROWS = 1024
TOKENS = 163840
N_NODE = 8
N_LOCAL = 16


def draw_hidden_acts(key, part):
    key = jax.random.fold_in(key, 11)
    first, second = jax.random.split(key, 2)
    power_table = jnp.array([0.125, 0.25, 0.5, 1.0, 2.0, 4.0], jnp.float32)
    digits = jax.random.randint(first, (TOKENS, ROWS), -8, 9)
    exponents = jax.random.randint(second, (ROWS,), 1, 6)
    scales = power_table[exponents]
    return (digits.astype(jnp.float32) * 0.25 * scales[None, :]).astype(jnp.bfloat16)


def draw_grad_out(key, part):
    key = jax.random.fold_in(key, 23)
    first, second = jax.random.split(key, 2)
    power_table = jnp.array([0.125, 0.25, 0.5, 1.0, 2.0, 4.0], jnp.float32)
    digits = jax.random.randint(first, (TOKENS, D), -8, 9)
    exponents = jax.random.randint(second, (D,), 1, 6)
    scales = power_table[exponents]
    return (digits.astype(jnp.float32) * (0.25 / 256.0) * scales[None, :]).astype(jnp.bfloat16)


def setup_inputs(seed: int = 0) -> dict:
    arg_keys = jax.random.split(jax.random.key(seed), 3)
    return {
        "hidden_acts": draw_hidden_acts(jax.random.fold_in(arg_keys[2], 71), 0),
        "grad_out": draw_grad_out(jax.random.fold_in(arg_keys[2], 71), 0),
    }


def unit_of(block_peak):
    power_two = jnp.full_like(block_peak, 2.0 ** -64)
    for exponent in (64, 32, 16, 8, 4, 2, 1):
        candidate = power_two * (2.0 ** exponent)
        power_two = jnp.where(candidate <= block_peak, candidate, power_two)
    return power_two / 64.0


def quantize(values):
    blocked = values.reshape(values.shape[:-1] + (values.shape[-1] // QB, QB))
    block_peak = jnp.max(jnp.abs(blocked), axis=-1, keepdims=True)
    block_unit = unit_of(block_peak)
    levels = jnp.clip(jnp.floor(blocked / block_unit + 0.5), -127.0, 127.0)
    return (levels * block_unit).astype(jnp.bfloat16).reshape(values.shape)


def reference(hidden_acts, grad_out):
    hidden_view = hidden_acts.reshape(N_NODE, N_LOCAL, TOK_DEV, ROWS)
    grad_view = grad_out.reshape(N_NODE, N_LOCAL, TOK_DEV, D)
    zero_sum = jnp.zeros((ROWS, D), jnp.float32)

    def node_step(running, node_inputs):
        def device_step(accumulated, device_inputs):
            partial_value = jnp.dot(device_inputs[0].T, device_inputs[1], preferred_element_type=jnp.float32)
            return accumulated + quantize(partial_value).astype(jnp.float32), None

        node_total, unused = lax.scan(device_step, zero_sum, node_inputs)
        return running + quantize(node_total).astype(jnp.float32), None

    summed, unused = lax.scan(node_step, zero_sum, (hidden_view, grad_view))
    return summed
```

```python
import functools

import jax
import jax.numpy as jnp
from jax import lax
from jax.experimental import pallas as pl
from jax.experimental.pallas import tpu as pltpu
from jax.sharding import PartitionSpec as P

QB = 128
NY, NX, NC = 4, 2, 2
N_NODE = 8
NODE_A = 3
NODE_B = N_NODE - NODE_A
ROWS_A, ROWS_B = 8 * NODE_A, 8 * NODE_B
SEC_A, SEC_B = NX * NY * ROWS_A, NX * NY * ROWS_B
HALF = SEC_A + SEC_B
COLS = 256
SLOTS = 8
LAG = (1, 3, 5, 7, 9)
MESH = pl.DeviceIdType.MESH
F32, BF16 = jnp.float32, jnp.bfloat16


def quantize(values):
    peak = jnp.max(jnp.abs(values), axis=-1, keepdims=True)
    scaled = peak * (2.0**23 + 1.0)
    power = scaled - scaled * (1.0 - 2.0**-24)
    power = jnp.minimum(jnp.maximum(power, 2.0**-64), 2.0**63)
    levels = jnp.floor(values * (64.0 / power) + 0.5)
    return jnp.minimum(jnp.maximum(levels, -127.0), 127.0) * (power * (1.0 / 64.0))


def kernel(
    chunks, ht, grad, out,
    gbuf, qsend, qrecv, sa, sb, xa, y1a, y2a, y1b, y2b, xb, ns, nr,
    gsem, core_s, core_r, x_s, x_r, y1_s, y1_r, y2_s, y2_r, node_s, node_r,
):
    me = lax.axis_index("node")
    loc = lax.axis_index("local")
    c, x, y = loc % NC, (loc // NC) % NX, loc // (NC * NX)
    up, down, far = (y + 1) % NY, (y + NY - 1) % NY, (y + 2) % NY
    sibling = {"local": loc + 1 - 2 * c}
    across = {"local": loc + NC * (1 - 2 * x)}
    above = {"local": (up * NX + x) * NC + c}
    below = {"local": (down * NX + x) * NC + c}
    other = 1 - x
    half = COLS // 2

    def remote(src, dst, s, r, device):
        return pltpu.make_async_remote_copy(
            src_ref=src, dst_ref=dst, send_sem=s, recv_sem=r, device_id=device, device_id_type=MESH
        )

    def load(t):
        cols = pl.ds(pl.multiple_of(t * COLS, COLS), COLS)
        return pltpu.make_async_copy(grad.at[:, cols], gbuf.at[t % 3], gsem.at[t % 3])

    def core_copy(t):
        return remote(qsend.at[t % 4], qrecv.at[t], core_s.at[t % SLOTS], core_r.at[t % SLOTS], sibling)

    def x_copies(t):
        k = t % SLOTS
        return (
            remote(sa.at[t, other], xa.at[t], x_s.at[k, 0], x_r.at[k, 0], across),
            remote(sb.at[t, y, other], xb.at[t], x_s.at[k, 1], x_r.at[k, 1], across),
        )

    def y1_copies(t):
        k = t % SLOTS
        made = []
        for i, (src, dst) in enumerate(((sa.at[t, x, far], y1a), (sb.at[t, far], y1b))):
            for d, device in enumerate((above, below)):
                made.append(
                    remote(
                        src.at[..., pl.ds(d * half, half)], dst.at[t, d],
                        y1_s.at[k, i, d], y1_r.at[k, i, d], device,
                    )
                )
        return made[:2], made[2:]

    def y2_copies(t):
        k = t % SLOTS
        made = []
        for i in range(2):
            for d, (row, device) in enumerate(((up, above), (down, below))):
                src = (sa.at[t, x, row], sb.at[t, row])[i]
                made.append(
                    remote(src, (y2a, y2b)[i].at[t, d], y2_s.at[k, i, d], y2_r.at[k, i, d], device)
                )
        return made[:2], made[2:]

    def node_send(t, k):
        to = (me + k) % N_NODE
        return remote(
            ns.at[t, to], nr.at[t, me], node_s.at[t % SLOTS, k], node_r.at[t % SLOTS, k], {"node": to}
        )

    def node_recv(t, k):
        source = (me + N_NODE - k) % N_NODE
        return remote(
            ns.at[t, source], nr.at[t, source],
            node_s.at[t % SLOTS, k], node_r.at[t % SLOTS, k], {"node": source},
        )

    def start(copies):
        for copy in copies:
            copy.start()

    def wait(copies):
        for copy in copies:
            copy.wait()

    barrier = pltpu.get_barrier_semaphore()
    peers = [sibling, across, above, below] + [{"node": (me + k) % N_NODE} for k in range(1, N_NODE)]
    load(0).start()
    load(1).start()
    for peer in peers:
        pl.semaphore_signal(barrier, inc=1, device_id=peer, device_id_type=MESH)
    pl.semaphore_wait(barrier, len(peers))

    def compute(t):
        @pl.when(t + 2 < chunks)
        def _():
            load(t + 2).start()

        load(t).wait()

        @pl.when(t >= 4)
        def _():
            core_copy(t - 4).wait_send()

        block = gbuf.at[t % 3]
        for first, count in ((0, 256), (256, 256)):
            rows = pl.ds(pl.multiple_of((1 - c) * HALF + first, 64), count)
            part = jnp.dot(ht[rows, :], block[...], preferred_element_type=F32)
            for j in range(COLS // QB):
                cut = slice(j * QB, (j + 1) * QB)
                qsend[t % 4, first : first + count, cut] = quantize(part[:, cut]).astype(BF16)
        core_copy(t).start()
        for first, count, dst, shape in (
            (0, SEC_A, sa, (NX, NY, ROWS_A, QB)),
            (SEC_A, SEC_B, sb, (NY, NX, ROWS_B, QB)),
        ):
            rows = pl.ds(pl.multiple_of(c * HALF + first, 64), count)
            part = jnp.dot(ht[rows, :], block[...], preferred_element_type=F32)
            for j in range(COLS // QB):
                cut = slice(j * QB, (j + 1) * QB)
                dst[t, :, :, :, cut] = quantize(part[:, cut]).reshape(shape)

    def stage1(t):
        core_copy(t).wait_recv()
        sa[t] = sa[t] + qrecv[t, :SEC_A].astype(F32).reshape(NX, NY, ROWS_A, COLS)
        x_copies(t)[0].start()
        sb[t] = sb[t] + qrecv[t, SEC_A:].astype(F32).reshape(NY, NX, ROWS_B, COLS)
        start(y1_copies(t)[1])

    def stage2(t):
        x_copies(t)[0].wait()
        sa[t, x] = sa[t, x] + xa[t]
        start(y1_copies(t)[0])
        wait(y1_copies(t)[1])
        sb[t, up, :, :, :half] = sb[t, up, :, :, :half] + y1b[t, 0]
        sb[t, down, :, :, half:] = sb[t, down, :, :, half:] + y1b[t, 1]
        start(y2_copies(t)[1])

    def stage3(t):
        wait(y1_copies(t)[0])
        sa[t, x, up, :, :half] = sa[t, x, up, :, :half] + y1a[t, 0]
        sa[t, x, down, :, half:] = sa[t, x, down, :, half:] + y1a[t, 1]
        start(y2_copies(t)[0])
        wait(y2_copies(t)[1])
        sb[t, y] = sb[t, y] + y2b[t, 0] + y2b[t, 1]
        x_copies(t)[1].start()

    def stage4(t):
        wait(y2_copies(t)[0])
        sum_a = sa[t, x, y] + y2a[t, 0] + y2a[t, 1]
        x_copies(t)[1].wait()
        sum_b = sb[t, y, x] + xb[t]
        for total, node, count in ((sum_a, 0, NODE_A), (sum_b, NODE_A, NODE_B)):
            pieces = [
                quantize(total[:, j * QB : (j + 1) * QB]).reshape(count, 8, QB) for j in range(COLS // QB)
            ]
            ns[t, node : node + count] = jnp.concatenate(pieces, axis=1).astype(BF16)
        for k in range(1, N_NODE):
            node_send(t, k).start()

    def stage5(t):
        total = ns[t, me].astype(F32)
        for k in range(1, N_NODE):
            node_send(t, k).wait_send()
            node_recv(t, k).wait_recv()
            total = total + nr[t, (me + N_NODE - k) % N_NODE].astype(F32)
        for j in range(COLS // QB):
            cols = pl.ds(pl.multiple_of(t * COLS + j * QB, QB), QB)
            out[:, cols] = total[8 * j : 8 * j + 8]

    def step(t, carry):
        pl.when(t < chunks)(lambda: compute(t))
        for lag, stage in zip(LAG, (stage1, stage2, stage3, stage4, stage5)):
            pl.when((t >= lag) & (t < chunks + lag))(functools.partial(stage, t - lag))
        return carry

    lax.fori_loop(0, chunks + LAG[-1], step, 0)
    for t in range(chunks - 4, chunks):
        core_copy(t).wait_send()


def per_device(hidden_acts, grad_out):
    tokens, width = grad_out.shape
    chunks = width // COLS
    blocked = hidden_acts.T.reshape(N_NODE, NY, NX, NC, 8, tokens)
    first = blocked[:NODE_A].transpose(3, 2, 1, 0, 4, 5).reshape(NC, SEC_A, tokens)
    second = blocked[NODE_A:].transpose(3, 1, 2, 0, 4, 5).reshape(NC, SEC_B, tokens)
    ht = jnp.concatenate([first, second], axis=1).reshape(NC * HALF, tokens)
    half = COLS // 2
    vmem, dma = pltpu.VMEM, pltpu.SemaphoreType.DMA
    return pl.pallas_call(
        functools.partial(kernel, chunks),
        out_shape=jax.ShapeDtypeStruct((8, width), F32),
        in_specs=[pl.BlockSpec(memory_space=pltpu.VMEM), pl.BlockSpec(memory_space=pl.ANY)],
        out_specs=pl.BlockSpec(memory_space=pltpu.VMEM),
        scratch_shapes=[
            vmem((3, tokens, COLS), BF16),
            vmem((4, HALF, COLS), BF16),
            vmem((chunks, HALF, COLS), BF16),
            vmem((chunks, NX, NY, ROWS_A, COLS), F32),
            vmem((chunks, NY, NX, ROWS_B, COLS), F32),
            vmem((chunks, NY, ROWS_A, COLS), F32),
            vmem((chunks, 2, ROWS_A, half), F32),
            vmem((chunks, 2, ROWS_A, COLS), F32),
            vmem((chunks, 2, NX, ROWS_B, half), F32),
            vmem((chunks, 2, NX, ROWS_B, COLS), F32),
            vmem((chunks, ROWS_B, COLS), F32),
            vmem((chunks, N_NODE, 16, half), BF16),
            vmem((chunks, N_NODE, 16, half), BF16),
            dma((3,)),
            dma((SLOTS,)),
            dma((SLOTS,)),
            dma((SLOTS, 2)),
            dma((SLOTS, 2)),
            dma((SLOTS, 2, 2)),
            dma((SLOTS, 2, 2)),
            dma((SLOTS, 2, 2)),
            dma((SLOTS, 2, 2)),
            dma((SLOTS, N_NODE)),
            dma((SLOTS, N_NODE)),
        ],
        compiler_params=pltpu.CompilerParams(
            collective_id=0, has_side_effects=True, vmem_limit_bytes=58 * 2**20
        ),
        cost_estimate=pl.CostEstimate(
            flops=2 * tokens * NC * HALF * width, bytes_accessed=2 * tokens * (width + NC * HALF), transcendentals=0
        ),
    )(ht, grad_out)


def solution(mesh):
    return jax.shard_map(
        per_device,
        mesh=mesh,
        in_specs=(P(("node", "local"), None), P(("node", "local"), None)),
        out_specs=P(("node", "local"), None),
        check_vma=False,
    )
```

```python
import functools

import jax
import jax.numpy as jnp
from jax import lax
from jax.experimental import pallas as pl
from jax.experimental.pallas import tpu as pltpu
from jax.sharding import PartitionSpec as P

QB = 128
NY, NX, NC = 4, 2, 2
N_NODE = 8
NODE_A = 3
NODE_B = N_NODE - NODE_A
ROWS_A, ROWS_B = 8 * NODE_A, 8 * NODE_B
SEC_A, SEC_B = NX * NY * ROWS_A, NX * NY * ROWS_B
HALF = SEC_A + SEC_B
COLS = 256
SLOTS = 8
LAG = (1, 3, 5, 7, 9)
MESH = pl.DeviceIdType.MESH
F32, BF16 = jnp.float32, jnp.bfloat16


def quantize(values):
    peak = jnp.max(jnp.abs(values), axis=-1, keepdims=True)
    scaled = peak * (2.0**23 + 1.0)
    power = scaled - scaled * (1.0 - 2.0**-24)
    power = jnp.minimum(jnp.maximum(power, 2.0**-64), 2.0**63)
    levels = jnp.floor(values * (64.0 / power) + 0.5)
    unit = power * (1.0 / 64.0)
    levels = jnp.minimum(jnp.maximum(levels, -127.0), 127.0)
    return levels * unit, jnp.where(peak > 0.0, unit, 2.0**57)


def wide_kernel(
    chunks, ht, grad, out,
    gbuf, qsend, qrecv, sa, sb, xa, y1a, y2a, y1b, y2b, xb, ns, nr,
    gsem, core_s, core_r, x_s, x_r, y1_s, y1_r, y2_s, y2_r, node_s, node_r,
):
    me = lax.axis_index("node")
    loc = lax.axis_index("local")
    c, x, y = loc % NC, (loc // NC) % NX, loc // (NC * NX)
    up, down, far = (y + 1) % NY, (y + NY - 1) % NY, (y + 2) % NY
    sibling = {"local": loc + 1 - 2 * c}
    across = {"local": loc + NC * (1 - 2 * x)}
    above = {"local": (up * NX + x) * NC + c}
    below = {"local": (down * NX + x) * NC + c}
    other = 1 - x
    half = COLS // 2

    def remote(src, dst, s, r, device):
        return pltpu.make_async_remote_copy(
            src_ref=src, dst_ref=dst, send_sem=s, recv_sem=r, device_id=device, device_id_type=MESH
        )

    def load(t):
        cols = pl.ds(pl.multiple_of(t * COLS, COLS), COLS)
        return pltpu.make_async_copy(grad.at[:, cols], gbuf.at[t % 3], gsem.at[t % 3])

    def core_copy(t):
        return remote(qsend.at[t % 4], qrecv.at[t], core_s.at[t % SLOTS], core_r.at[t % SLOTS], sibling)

    def x_copies(t):
        k = t % SLOTS
        return (
            remote(sa.at[t, other], xa.at[t], x_s.at[k, 0], x_r.at[k, 0], across),
            remote(sb.at[t, y, other], xb.at[t], x_s.at[k, 1], x_r.at[k, 1], across),
        )

    def y1_copies(t):
        k = t % SLOTS
        made = []
        for i, (src, dst) in enumerate(((sa.at[t, x, far], y1a), (sb.at[t, far], y1b))):
            for d, device in enumerate((above, below)):
                made.append(
                    remote(
                        src.at[..., pl.ds(d * half, half)], dst.at[t, d],
                        y1_s.at[k, i, d], y1_r.at[k, i, d], device,
                    )
                )
        return made[:2], made[2:]

    def y2_copies(t):
        k = t % SLOTS
        made = []
        for i in range(2):
            for d, (row, device) in enumerate(((up, above), (down, below))):
                src = (sa.at[t, x, row], sb.at[t, row])[i]
                made.append(
                    remote(src, (y2a, y2b)[i].at[t, d], y2_s.at[k, i, d], y2_r.at[k, i, d], device)
                )
        return made[:2], made[2:]

    def node_send(t, k):
        to = (me + k) % N_NODE
        return remote(
            ns.at[t, to], nr.at[t, me], node_s.at[t % SLOTS, k], node_r.at[t % SLOTS, k], {"node": to}
        )

    def node_recv(t, k):
        source = (me + N_NODE - k) % N_NODE
        return remote(
            ns.at[t, source], nr.at[t, source],
            node_s.at[t % SLOTS, k], node_r.at[t % SLOTS, k], {"node": source},
        )

    def start(copies):
        for copy in copies:
            copy.start()

    def wait(copies):
        for copy in copies:
            copy.wait()

    barrier = pltpu.get_barrier_semaphore()
    peers = [sibling, across, above, below] + [{"node": (me + k) % N_NODE} for k in range(1, N_NODE)]
    load(0).start()
    load(1).start()
    for peer in peers:
        pl.semaphore_signal(barrier, inc=1, device_id=peer, device_id_type=MESH)
    pl.semaphore_wait(barrier, len(peers))

    def compute(t):
        @pl.when(t + 2 < chunks)
        def _():
            load(t + 2).start()

        load(t).wait()

        @pl.when(t >= 4)
        def _():
            core_copy(t - 4).wait_send()

        block = gbuf.at[t % 3]
        for first, count in ((0, 256), (256, 256)):
            rows = pl.ds(pl.multiple_of((1 - c) * HALF + first, 64), count)
            part = jnp.dot(ht[rows, :], block[...], preferred_element_type=F32)
            for j in range(COLS // QB):
                cut = slice(j * QB, (j + 1) * QB)
                qsend[t % 4, first : first + count, cut] = quantize(part[:, cut])[0].astype(BF16)
        core_copy(t).start()
        for first, count, dst, shape in (
            (0, SEC_A, sa, (NX, NY, ROWS_A, QB)),
            (SEC_A, SEC_B, sb, (NY, NX, ROWS_B, QB)),
        ):
            rows = pl.ds(pl.multiple_of(c * HALF + first, 64), count)
            part = jnp.dot(ht[rows, :], block[...], preferred_element_type=F32)
            for j in range(COLS // QB):
                cut = slice(j * QB, (j + 1) * QB)
                dst[t, :, :, :, cut] = quantize(part[:, cut])[0].reshape(shape)

    def stage1(t):
        core_copy(t).wait_recv()
        sa[t] = sa[t] + qrecv[t, :SEC_A].astype(F32).reshape(NX, NY, ROWS_A, COLS)
        x_copies(t)[0].start()
        sb[t] = sb[t] + qrecv[t, SEC_A:].astype(F32).reshape(NY, NX, ROWS_B, COLS)
        start(y1_copies(t)[1])

    def stage2(t):
        x_copies(t)[0].wait()
        sa[t, x] = sa[t, x] + xa[t]
        start(y1_copies(t)[0])
        wait(y1_copies(t)[1])
        sb[t, up, :, :, :half] = sb[t, up, :, :, :half] + y1b[t, 0]
        sb[t, down, :, :, half:] = sb[t, down, :, :, half:] + y1b[t, 1]
        start(y2_copies(t)[1])

    def stage3(t):
        wait(y1_copies(t)[0])
        sa[t, x, up, :, :half] = sa[t, x, up, :, :half] + y1a[t, 0]
        sa[t, x, down, :, half:] = sa[t, x, down, :, half:] + y1a[t, 1]
        start(y2_copies(t)[0])
        wait(y2_copies(t)[1])
        sb[t, y] = sb[t, y] + y2b[t, 0] + y2b[t, 1]
        x_copies(t)[1].start()

    def stage4(t):
        wait(y2_copies(t)[0])
        sum_a = sa[t, x, y] + y2a[t, 0] + y2a[t, 1]
        x_copies(t)[1].wait()
        sum_b = sb[t, y, x] + xb[t]
        for total, node, count in ((sum_a, 0, NODE_A), (sum_b, NODE_A, NODE_B)):
            pieces = [
                quantize(total[:, j * QB : (j + 1) * QB])[0].reshape(count, 8, QB) for j in range(COLS // QB)
            ]
            ns[t, node : node + count] = jnp.concatenate(pieces, axis=1).astype(BF16)
        for k in range(1, N_NODE):
            node_send(t, k).start()

    def stage5(t):
        total = ns[t, me].astype(F32)
        for k in range(1, N_NODE):
            node_send(t, k).wait_send()
            node_recv(t, k).wait_recv()
            total = total + nr[t, (me + N_NODE - k) % N_NODE].astype(F32)
        for j in range(COLS // QB):
            cols = pl.ds(pl.multiple_of(t * COLS + j * QB, QB), QB)
            out[:, cols] = total[8 * j : 8 * j + 8]

    def step(t, carry):
        pl.when(t < chunks)(lambda: compute(t))
        for lag, stage in zip(LAG, (stage1, stage2, stage3, stage4, stage5)):
            pl.when((t >= lag) & (t < chunks + lag))(functools.partial(stage, t - lag))
        return carry

    lax.fori_loop(0, chunks + LAG[-1], step, 0)
    for t in range(chunks - 4, chunks):
        core_copy(t).wait_send()


def split_power(words):
    scaled = words * (2.0**23 + 1.0)
    return scaled - scaled * (1.0 - 2.0**-24)


def unpack(words):
    signed = split_power(words)
    both = words - signed
    scale = jnp.abs(signed)
    magic = scale * 6144.0
    first = (both + magic) - magic
    return first, both - first, scale


def packed_kernel(
    chunks, ht, grad, out, flag_out,
    gbuf, qsend, qrecv, own, sa, sb,
    xas, y1as, y2as, y1bs, y2bs, xbs, xa, y1a, y2a, y1b, y2b, xb, ns, nr, flag, fsend, frecv,
    gsem, core_s, core_r, x_s, x_r, y1_s, y1_r, y2_s, y2_r, node_s, node_r, flag_s, flag_r,
):
    me = lax.axis_index("node")
    loc = lax.axis_index("local")
    c, x, y = loc % NC, (loc // NC) % NX, loc // (NC * NX)
    far = (y + 2) % NY
    other = 1 - x

    def at_y(row):
        return {"local": (row * NX + x) * NC + c}

    sibling = {"local": loc + 1 - 2 * c}
    across = {"local": loc + NC * (1 - 2 * x)}
    ring = [at_y((y + k) % NY) for k in (1, 3, 2)]

    def remote(src, dst, s, r, device):
        return pltpu.make_async_remote_copy(
            src_ref=src, dst_ref=dst, send_sem=s, recv_sem=r, device_id=device, device_id_type=MESH
        )

    def load(t):
        cols = pl.ds(pl.multiple_of(t * COLS, COLS), COLS)
        return pltpu.make_async_copy(grad.at[:, cols], gbuf.at[t % 3], gsem.at[t % 3])

    def core_copy(t):
        return remote(qsend.at[t % 4], qrecv.at[t], core_s.at[t % SLOTS], core_r.at[t % SLOTS], sibling)

    def turn(t, part):
        odd = (t + part) % 2
        return (y + 1 + 2 * odd) % NY, (y + 3 - 2 * odd) % NY

    def xa_copy(t):
        k = t % SLOTS
        return remote(xas.at[k], xa.at[t], x_s.at[k, 0], x_r.at[k, 0], across)

    def xb_copy(t):
        k = t % SLOTS
        return remote(xbs.at[k], xb.at[t], x_s.at[k, 1], x_r.at[k, 1], across)

    def y1_copy(t, part):
        k = t % SLOTS
        src, dst = ((y1as, y1a), (y1bs, y1b))[part]
        return remote(src.at[k], dst.at[t], y1_s.at[k, part], y1_r.at[k, part], at_y(turn(t, part)[0]))

    def y2_copy(t, part, late):
        k = t % SLOTS
        src, dst = ((y2as, y2a), (y2bs, y2b))[part]
        return remote(
            src.at[k, late], dst.at[t, late], y2_s.at[k, part, late], y2_r.at[k, part, late],
            at_y(turn(t, part)[1 - late]),
        )

    def node_send(t, k):
        to = (me + k) % N_NODE
        return remote(
            ns.at[t % SLOTS, to], nr.at[t, me], node_s.at[t % SLOTS, k], node_r.at[t % SLOTS, k], {"node": to}
        )

    def node_recv(t, k):
        source = (me + N_NODE - k) % N_NODE
        return remote(
            ns.at[t % SLOTS, source], nr.at[t, source],
            node_s.at[t % SLOTS, k], node_r.at[t % SLOTS, k], {"node": source},
        )

    def pack(first, second, scale):
        both = first + second
        excess = jnp.maximum(jnp.abs(both), jnp.abs(second) * 4096.0) - scale
        flag[...] = jnp.maximum(flag[...], jnp.max(excess.reshape(-1, 8, QB), axis=0))
        return both + jnp.where(both < 0.0, -scale, scale)

    def join(left, right):
        return left[0] + right[0], left[1] + right[1], jnp.minimum(left[2], right[2])

    def rows_of(index, count):
        return pl.ds(pl.multiple_of(index * count, 8), count)

    barrier = pltpu.get_barrier_semaphore()
    peers = [sibling, across] + ring + [{"node": (me + k) % N_NODE} for k in range(1, N_NODE)]
    load(0).start()
    load(1).start()
    for peer in peers:
        pl.semaphore_signal(barrier, inc=1, device_id=peer, device_id_type=MESH)
    flag[...] = jnp.full((8, QB), -1.0, F32)
    pl.semaphore_wait(barrier, len(peers))

    def compute(t):
        @pl.when(t + 2 < chunks)
        def _():
            load(t + 2).start()

        load(t).wait()

        @pl.when(t >= 4)
        def _():
            core_copy(t - 4).wait_send()

        block = gbuf.at[t % 3]
        for mine in (0, 1):
            for first, count in ((0, 256), (256, 256)):
                start = (c if mine else 1 - c) * HALF + first
                rows = pl.ds(pl.multiple_of(start, 256), count)
                part = jnp.dot(ht[rows, :], block[...], preferred_element_type=F32)
                one, unit_one = quantize(part[:, :QB])
                two, unit_two = quantize(part[:, QB:])
                scale = jnp.minimum(unit_one, unit_two) * 2.0**23
                one = one * 4096.0
                if mine:
                    own[t % 2, 0, first : first + count] = one
                    own[t % 2, 1, first : first + count] = two
                    own[t % 2, 2, first : first + count] = jnp.broadcast_to(scale, (count, QB))
                else:
                    qsend[t % 4, first : first + count] = pack(one, two, scale)
            if not mine:
                core_copy(t).start()

    def stage1(t):
        k = t % SLOTS
        core_copy(t).wait_recv()

        def pair(first, index, count):
            rows = pl.ds(pl.multiple_of(first + index * count, 8), count)
            return join(unpack(qrecv[t, rows]), tuple(own[t % 2, i, rows] for i in range(3)))

        xas[k] = pack(*pair(0, other, NY * ROWS_A))
        xa_copy(t).start()
        ahead, behind = turn(t, 1)
        y1bs[k] = pack(*pair(SEC_A, far, NX * ROWS_B))
        y1_copy(t, 1).start()
        y2bs[k, 0] = pack(*pair(SEC_A, behind, NX * ROWS_B))
        y2_copy(t, 1, 0).start()
        for i, value in enumerate(pair(0, x, NY * ROWS_A)):
            sa[k, i] = value
        for j, row in enumerate((ahead, y)):
            for i, value in enumerate(pair(SEC_A, row, NX * ROWS_B)):
                sb[k, j, i] = value

    def stage2(t):
        k = t % SLOTS
        xa_copy(t).wait()

        def pair(row):
            rows = rows_of(row, ROWS_A)
            return join(unpack(xa[t, rows]), tuple(sa[k, i, rows] for i in range(3)))

        ahead, behind = turn(t, 0)
        y1as[k] = pack(*pair(far))
        y1_copy(t, 0).start()
        y2as[k, 0] = pack(*pair(behind))
        y2_copy(t, 0, 0).start()
        for row in (ahead, y):
            for i, value in enumerate(pair(row)):
                sa[k, i, rows_of(row, ROWS_A)] = value
        y1_copy(t, 1).wait()
        y2bs[k, 1] = pack(*join(unpack(y1b[t]), tuple(sb[k, 0, i] for i in range(3))))
        y2_copy(t, 1, 1).start()

    def stage3(t):
        k = t % SLOTS
        y1_copy(t, 0).wait()
        rows = rows_of(turn(t, 0)[0], ROWS_A)
        y2as[k, 1] = pack(*join(unpack(y1a[t]), tuple(sa[k, i, rows] for i in range(3))))
        y2_copy(t, 0, 1).start()
        y2_copy(t, 1, 0).wait()
        y2_copy(t, 1, 1).wait()

        def pair(index):
            rows = rows_of(index, ROWS_B)
            held = tuple(sb[k, 1, i, rows] for i in range(3))
            return join(join(unpack(y2b[t, 0, rows]), unpack(y2b[t, 1, rows])), held)

        xbs[k] = pack(*pair(other))
        xb_copy(t).start()
        for i, value in enumerate(pair(x)[:2]):
            sb[k, 0, i, :ROWS_B] = value

    def stage4(t):
        k = t % SLOTS
        y2_copy(t, 0, 0).wait()
        y2_copy(t, 0, 1).wait()
        rows = rows_of(y, ROWS_A)
        left, right = unpack(y2a[t, 0]), unpack(y2a[t, 1])
        sum_a = [sa[k, i, rows] + left[i] + right[i] for i in range(2)]
        xb_copy(t).wait()
        last = unpack(xb[t])
        sum_b = [sb[k, 0, i, :ROWS_B] + last[i] for i in range(2)]
        for total, node, count in ((sum_a, 0, NODE_A), (sum_b, NODE_A, NODE_B)):
            pieces = [
                quantize(total[0] * (1.0 / 4096.0))[0].reshape(count, 8, QB),
                quantize(total[1])[0].reshape(count, 8, QB),
            ]
            ns[k, node : node + count] = jnp.concatenate(pieces, axis=1).astype(BF16)
        for j in range(1, N_NODE):
            node_send(t, j).start()

    def stage5(t):
        total = ns[t % SLOTS, me].astype(F32)
        for j in range(1, N_NODE):
            node_send(t, j).wait_send()
            node_recv(t, j).wait_recv()
            total = total + nr[t, (me + N_NODE - j) % N_NODE].astype(F32)
        for j in range(COLS // QB):
            cols = pl.ds(pl.multiple_of(t * COLS + j * QB, QB), QB)
            out[:, cols] = total[8 * j : 8 * j + 8]

    rounds = ([sibling], [across], ring, [{"node": (me + k) % N_NODE} for k in range(1, N_NODE)])
    places = (0, 1, 2, 5)

    def flag_copies(index):
        return [
            remote(
                fsend.at[index], frecv.at[places[index] + i],
                flag_s.at[places[index] + i], flag_r.at[places[index] + i], device,
            )
            for i, device in enumerate(rounds[index])
        ]

    def flag_round(index):
        value = flag[...] if index == 0 else fsend[index - 1]
        if index:
            for i, copy in enumerate(flag_copies(index - 1)):
                copy.wait()
                value = jnp.maximum(value, frecv[places[index - 1] + i])
        if index == len(rounds):
            flag_out[...] = value
            return
        fsend[index] = value
        for copy in flag_copies(index):
            copy.start()

    def step(t, carry):
        pl.when(t < chunks)(lambda: compute(t))
        for lag, stage in zip(LAG, (stage1, stage2, stage3, stage4, stage5)):
            pl.when((t >= lag) & (t < chunks + lag))(functools.partial(stage, t - lag))
        for index in range(len(rounds)):
            pl.when(t == chunks + LAG[2] + index)(functools.partial(flag_round, index))
        return carry

    lax.fori_loop(0, chunks + LAG[-1], step, 0)
    flag_round(len(rounds))
    for t in range(chunks - 4, chunks):
        core_copy(t).wait_send()


def arrange(hidden_acts):
    tokens = hidden_acts.shape[0]
    blocked = hidden_acts.T.reshape(N_NODE, NY, NX, NC, 8, tokens)
    first = blocked[:NODE_A].transpose(3, 2, 1, 0, 4, 5).reshape(NC, SEC_A, tokens)
    second = blocked[NODE_A:].transpose(3, 1, 2, 0, 4, 5).reshape(NC, SEC_B, tokens)
    return jnp.concatenate([first, second], axis=1).reshape(NC * HALF, tokens)


def call(body, collective_id, ht, grad_out, extra_out, scratch):
    tokens, width = grad_out.shape
    vmem_spec = pl.BlockSpec(memory_space=pltpu.VMEM)
    out_shape = [jax.ShapeDtypeStruct((8, width), F32)] + extra_out
    return pl.pallas_call(
        functools.partial(body, width // COLS),
        out_shape=out_shape,
        in_specs=[vmem_spec, pl.BlockSpec(memory_space=pl.ANY)],
        out_specs=[vmem_spec] * len(out_shape),
        scratch_shapes=scratch,
        compiler_params=pltpu.CompilerParams(
            collective_id=collective_id, has_side_effects=True, vmem_limit_bytes=58 * 2**20
        ),
        cost_estimate=pl.CostEstimate(
            flops=2 * tokens * NC * HALF * width, bytes_accessed=2 * tokens * (width + NC * HALF), transcendentals=0
        ),
    )(ht, grad_out)


def wide(ht, grad_out):
    tokens, width = grad_out.shape
    chunks, half = width // COLS, COLS // 2
    vmem, dma = pltpu.VMEM, pltpu.SemaphoreType.DMA
    scratch = [
        vmem((3, tokens, COLS), BF16),
        vmem((4, HALF, COLS), BF16),
        vmem((chunks, HALF, COLS), BF16),
        vmem((chunks, NX, NY, ROWS_A, COLS), F32),
        vmem((chunks, NY, NX, ROWS_B, COLS), F32),
        vmem((chunks, NY, ROWS_A, COLS), F32),
        vmem((chunks, 2, ROWS_A, half), F32),
        vmem((chunks, 2, ROWS_A, COLS), F32),
        vmem((chunks, 2, NX, ROWS_B, half), F32),
        vmem((chunks, 2, NX, ROWS_B, COLS), F32),
        vmem((chunks, ROWS_B, COLS), F32),
        vmem((chunks, N_NODE, 16, half), BF16),
        vmem((chunks, N_NODE, 16, half), BF16),
        dma((3,)),
        *[dma((SLOTS,))] * 2,
        *[dma((SLOTS, 2))] * 2,
        *[dma((SLOTS, 2, 2))] * 4,
        *[dma((SLOTS, N_NODE))] * 2,
    ]
    return call(wide_kernel, 1, ht, grad_out, [], scratch)[0]


def packed(ht, grad_out):
    tokens, width = grad_out.shape
    chunks = width // COLS
    vmem, dma = pltpu.VMEM, pltpu.SemaphoreType.DMA
    sizes = [(NY * ROWS_A,), (ROWS_A,), (2, ROWS_A), (NX * ROWS_B,), (2, NX * ROWS_B), (ROWS_B,)]
    scratch = [
        vmem((3, tokens, COLS), BF16),
        vmem((4, HALF, QB), F32),
        vmem((chunks, HALF, QB), F32),
        vmem((2, 3, HALF, QB), F32),
        vmem((SLOTS, 3, NY * ROWS_A, QB), F32),
        vmem((SLOTS, 2, 3, NX * ROWS_B, QB), F32),
        *[vmem((SLOTS, *size, QB), F32) for size in sizes],
        *[vmem((chunks, *size, QB), F32) for size in sizes],
        vmem((SLOTS, N_NODE, 16, QB), BF16),
        vmem((chunks, N_NODE, 16, QB), BF16),
        vmem((8, QB), F32),
        vmem((4, 8, QB), F32),
        vmem((12, 8, QB), F32),
        dma((3,)),
        *[dma((SLOTS,))] * 2,
        *[dma((SLOTS, 2))] * 4,
        *[dma((SLOTS, 2, 2))] * 2,
        *[dma((SLOTS, N_NODE))] * 2,
        *[dma((12,))] * 2,
    ]
    out, flag = call(packed_kernel, 0, ht, grad_out, [jax.ShapeDtypeStruct((8, QB), F32)], scratch)
    return out, jnp.max(flag) >= 0.0


def per_device(hidden_acts, grad_out):
    ht = arrange(hidden_acts)
    out, misfit = packed(ht, grad_out)
    return lax.cond(misfit, lambda: wide(ht, grad_out), lambda: out)


def solution(mesh):
    return jax.shard_map(
        per_device,
        mesh=mesh,
        in_specs=(P(("node", "local"), None), P(("node", "local"), None)),
        out_specs=P(("node", "local"), None),
        check_vma=False,
    )
```

```python
import functools

import jax
import jax.numpy as jnp
from jax import lax
from jax.experimental import pallas as pl
from jax.experimental.pallas import tpu as pltpu
from jax.sharding import PartitionSpec as P

QB = 128
NY, NX, NC = 4, 2, 2
N_NODE = 8
NODE_A = 3
NODE_B = N_NODE - NODE_A
ROWS_A, ROWS_B = 8 * NODE_A, 8 * NODE_B
SEC_A, SEC_B = NX * NY * ROWS_A, NX * NY * ROWS_B
HALF = SEC_A + SEC_B
COLS = 256
SPAN = 512
WORDS = SPAN // 2
SLOTS = 8
PACKED_LAG = (0, 1, 2, 4, 5, 7)
LAG = (1, 3, 5, 7, 9)
MESH = pl.DeviceIdType.MESH
F32, BF16 = jnp.float32, jnp.bfloat16


def quantize(values):
    peak = jnp.max(jnp.abs(values), axis=-1, keepdims=True)
    scaled = peak * (2.0**23 + 1.0)
    power = scaled - scaled * (1.0 - 2.0**-24)
    power = jnp.minimum(jnp.maximum(power, 2.0**-64), 2.0**63)
    levels = jnp.floor(values * (64.0 / power) + 0.5)
    unit = power * (1.0 / 64.0)
    levels = jnp.minimum(jnp.maximum(levels, -127.0), 127.0)
    return levels * unit, jnp.where(peak > 0.0, unit, 2.0**57)


def wide_kernel(
    chunks, ht, grad, out,
    gbuf, qsend, qrecv, sa, sb, xa, y1a, y2a, y1b, y2b, xb, ns, nr,
    gsem, core_s, core_r, x_s, x_r, y1_s, y1_r, y2_s, y2_r, node_s, node_r,
):
    me = lax.axis_index("node")
    loc = lax.axis_index("local")
    c, x, y = loc % NC, (loc // NC) % NX, loc // (NC * NX)
    up, down, far = (y + 1) % NY, (y + NY - 1) % NY, (y + 2) % NY
    sibling = {"local": loc + 1 - 2 * c}
    across = {"local": loc + NC * (1 - 2 * x)}
    above = {"local": (up * NX + x) * NC + c}
    below = {"local": (down * NX + x) * NC + c}
    other = 1 - x
    half = COLS // 2

    def remote(src, dst, s, r, device):
        return pltpu.make_async_remote_copy(
            src_ref=src, dst_ref=dst, send_sem=s, recv_sem=r, device_id=device, device_id_type=MESH
        )

    def load(t):
        cols = pl.ds(pl.multiple_of(t * COLS, COLS), COLS)
        return pltpu.make_async_copy(grad.at[:, cols], gbuf.at[t % 3], gsem.at[t % 3])

    def core_copy(t):
        return remote(qsend.at[t % 4], qrecv.at[t], core_s.at[t % SLOTS], core_r.at[t % SLOTS], sibling)

    def x_copies(t):
        k = t % SLOTS
        return (
            remote(sa.at[t, other], xa.at[t], x_s.at[k, 0], x_r.at[k, 0], across),
            remote(sb.at[t, y, other], xb.at[t], x_s.at[k, 1], x_r.at[k, 1], across),
        )

    def y1_copies(t):
        k = t % SLOTS
        made = []
        for i, (src, dst) in enumerate(((sa.at[t, x, far], y1a), (sb.at[t, far], y1b))):
            for d, device in enumerate((above, below)):
                made.append(
                    remote(
                        src.at[..., pl.ds(d * half, half)], dst.at[t, d],
                        y1_s.at[k, i, d], y1_r.at[k, i, d], device,
                    )
                )
        return made[:2], made[2:]

    def y2_copies(t):
        k = t % SLOTS
        made = []
        for i in range(2):
            for d, (row, device) in enumerate(((up, above), (down, below))):
                src = (sa.at[t, x, row], sb.at[t, row])[i]
                made.append(
                    remote(src, (y2a, y2b)[i].at[t, d], y2_s.at[k, i, d], y2_r.at[k, i, d], device)
                )
        return made[:2], made[2:]

    def node_send(t, k):
        to = (me + k) % N_NODE
        return remote(
            ns.at[t, to], nr.at[t, me], node_s.at[t % SLOTS, k], node_r.at[t % SLOTS, k], {"node": to}
        )

    def node_recv(t, k):
        source = (me + N_NODE - k) % N_NODE
        return remote(
            ns.at[t, source], nr.at[t, source],
            node_s.at[t % SLOTS, k], node_r.at[t % SLOTS, k], {"node": source},
        )

    def start(copies):
        for copy in copies:
            copy.start()

    def wait(copies):
        for copy in copies:
            copy.wait()

    barrier = pltpu.get_barrier_semaphore()
    peers = [sibling, across, above, below] + [{"node": (me + k) % N_NODE} for k in range(1, N_NODE)]
    load(0).start()
    load(1).start()
    for peer in peers:
        pl.semaphore_signal(barrier, inc=1, device_id=peer, device_id_type=MESH)
    pl.semaphore_wait(barrier, len(peers))

    def compute(t):
        @pl.when(t + 2 < chunks)
        def _():
            load(t + 2).start()

        load(t).wait()

        @pl.when(t >= 4)
        def _():
            core_copy(t - 4).wait_send()

        block = gbuf.at[t % 3]
        for first, count in ((0, 256), (256, 256)):
            rows = pl.ds(pl.multiple_of((1 - c) * HALF + first, 64), count)
            part = jnp.dot(ht[rows, :], block[...], preferred_element_type=F32)
            for j in range(COLS // QB):
                cut = slice(j * QB, (j + 1) * QB)
                qsend[t % 4, first : first + count, cut] = quantize(part[:, cut])[0].astype(BF16)
        core_copy(t).start()
        for first, count, dst, shape in (
            (0, SEC_A, sa, (NX, NY, ROWS_A, QB)),
            (SEC_A, SEC_B, sb, (NY, NX, ROWS_B, QB)),
        ):
            rows = pl.ds(pl.multiple_of(c * HALF + first, 64), count)
            part = jnp.dot(ht[rows, :], block[...], preferred_element_type=F32)
            for j in range(COLS // QB):
                cut = slice(j * QB, (j + 1) * QB)
                dst[t, :, :, :, cut] = quantize(part[:, cut])[0].reshape(shape)

    def stage1(t):
        core_copy(t).wait_recv()
        sa[t] = sa[t] + qrecv[t, :SEC_A].astype(F32).reshape(NX, NY, ROWS_A, COLS)
        x_copies(t)[0].start()
        sb[t] = sb[t] + qrecv[t, SEC_A:].astype(F32).reshape(NY, NX, ROWS_B, COLS)
        start(y1_copies(t)[1])

    def stage2(t):
        x_copies(t)[0].wait()
        sa[t, x] = sa[t, x] + xa[t]
        start(y1_copies(t)[0])
        wait(y1_copies(t)[1])
        sb[t, up, :, :, :half] = sb[t, up, :, :, :half] + y1b[t, 0]
        sb[t, down, :, :, half:] = sb[t, down, :, :, half:] + y1b[t, 1]
        start(y2_copies(t)[1])

    def stage3(t):
        wait(y1_copies(t)[0])
        sa[t, x, up, :, :half] = sa[t, x, up, :, :half] + y1a[t, 0]
        sa[t, x, down, :, half:] = sa[t, x, down, :, half:] + y1a[t, 1]
        start(y2_copies(t)[0])
        wait(y2_copies(t)[1])
        sb[t, y] = sb[t, y] + y2b[t, 0] + y2b[t, 1]
        x_copies(t)[1].start()

    def stage4(t):
        wait(y2_copies(t)[0])
        sum_a = sa[t, x, y] + y2a[t, 0] + y2a[t, 1]
        x_copies(t)[1].wait()
        sum_b = sb[t, y, x] + xb[t]
        for total, node, count in ((sum_a, 0, NODE_A), (sum_b, NODE_A, NODE_B)):
            pieces = [
                quantize(total[:, j * QB : (j + 1) * QB])[0].reshape(count, 8, QB) for j in range(COLS // QB)
            ]
            ns[t, node : node + count] = jnp.concatenate(pieces, axis=1).astype(BF16)
        for k in range(1, N_NODE):
            node_send(t, k).start()

    def stage5(t):
        total = ns[t, me].astype(F32)
        for k in range(1, N_NODE):
            node_send(t, k).wait_send()
            node_recv(t, k).wait_recv()
            total = total + nr[t, (me + N_NODE - k) % N_NODE].astype(F32)
        for j in range(COLS // QB):
            cols = pl.ds(pl.multiple_of(t * COLS + j * QB, QB), QB)
            out[:, cols] = total[8 * j : 8 * j + 8]

    def step(t, carry):
        pl.when(t < chunks)(lambda: compute(t))
        for lag, stage in zip(LAG, (stage1, stage2, stage3, stage4, stage5)):
            pl.when((t >= lag) & (t < chunks + lag))(functools.partial(stage, t - lag))
        return carry

    lax.fori_loop(0, chunks + LAG[-1], step, 0)
    for t in range(chunks - 4, chunks):
        core_copy(t).wait_send()


def split_power(words):
    scaled = words * (2.0**23 + 1.0)
    return scaled - scaled * (1.0 - 2.0**-24)


def unpack(words):
    signed = split_power(words)
    both = words - signed
    scale = jnp.abs(signed)
    magic = scale * 6144.0
    first = (both + magic) - magic
    return first, both - first, scale


def packed_kernel(
    chunks, ht, grad, out, flag_out,
    gbuf, qsend, qrecv, own, sa, sb,
    xas, y1as, y2as, y1bs, y2bs, xbs, xa, y1a, y2a, y1b, y2b, xb, ns, nr, flag, fsend, frecv,
    gsem, core_s, core_r, x_s, x_r, y1_s, y1_r, y2_s, y2_r, node_s, node_r, flag_s, flag_r,
):
    me = lax.axis_index("node")
    loc = lax.axis_index("local")
    c, x, y = loc % NC, (loc // NC) % NX, loc // (NC * NX)
    far = (y + 2) % NY
    other = 1 - x

    def at_y(row):
        return {"local": (row * NX + x) * NC + c}

    sibling = {"local": loc + 1 - 2 * c}
    across = {"local": loc + NC * (1 - 2 * x)}
    near = [sibling, across, {"local": loc + 1 - 2 * c + NC * (1 - 2 * x)}]
    ring = [at_y((y + k) % NY) for k in (1, 3, 2)]

    def remote(src, dst, s, r, device):
        return pltpu.make_async_remote_copy(
            src_ref=src, dst_ref=dst, send_sem=s, recv_sem=r, device_id=device, device_id_type=MESH
        )

    def load(t):
        cols = pl.ds(pl.multiple_of(t * SPAN, SPAN), SPAN)
        return pltpu.make_async_copy(grad.at[:, cols], gbuf.at[t % 3], gsem.at[t % 3])

    def core_copy(t):
        return remote(qsend.at[t % 4], qrecv.at[t], core_s.at[t % SLOTS], core_r.at[t % SLOTS], sibling)

    def turn(t, part):
        odd = (t + part) % 2
        return (y + 1 + 2 * odd) % NY, (y + 3 - 2 * odd) % NY

    def xa_copy(t):
        k = t % SLOTS
        return remote(xas.at[k], xa.at[t], x_s.at[k, 0], x_r.at[k, 0], across)

    def xb_copy(t):
        k = t % SLOTS
        return remote(xbs.at[k], xb.at[t], x_s.at[k, 1], x_r.at[k, 1], across)

    def y1_copy(t, part):
        k = t % SLOTS
        src, dst = ((y1as, y1a), (y1bs, y1b))[part]
        return remote(src.at[k], dst.at[t], y1_s.at[k, part], y1_r.at[k, part], at_y(turn(t, part)[0]))

    def y2_copy(t, part, late):
        k = t % SLOTS
        src, dst = ((y2as, y2a), (y2bs, y2b))[part]
        return remote(
            src.at[k, late], dst.at[t, late], y2_s.at[k, part, late], y2_r.at[k, part, late],
            at_y(turn(t, part)[1 - late]),
        )

    def node_send(group, j):
        to = (me + j) % N_NODE
        k = group % SLOTS
        return remote(ns.at[k, to], nr.at[group, me], node_s.at[k], node_r.at[k], {"node": to})

    def node_all(group):
        k, count = group % SLOTS, pl.ds(0, N_NODE - 1)
        return remote(ns.at[k, count], nr.at[group, count], node_s.at[k], node_r.at[k], {"node": (me + 1) % N_NODE})

    def pack(first, second, scale):
        both = first + second
        excess = jnp.maximum(jnp.abs(both), jnp.abs(second) * 4096.0) - scale
        width = scale.shape[-1]
        flag[:, :width] = jnp.maximum(flag[:, :width], jnp.max(excess.reshape(-1, 8, width), axis=0))
        return both + jnp.where(both < 0.0, -scale, scale)

    def join(left, right):
        return left[0] + right[0], left[1] + right[1], jnp.minimum(left[2], right[2])

    def rows_of(index, count):
        return pl.ds(pl.multiple_of(index * count, 8), count)

    barrier = pltpu.get_barrier_semaphore()
    peers = near + ring + [{"node": (me + k) % N_NODE} for k in range(1, N_NODE)]
    load(0).start()
    load(1).start()
    for peer in peers:
        pl.semaphore_signal(barrier, inc=1, device_id=peer, device_id_type=MESH)
    flag[...] = jnp.full((8, WORDS), -1.0, F32)

    def compute(t, mine):
        for first in range(0, HALF, 256):
            start = (c if mine else 1 - c) * HALF + first
            rows = pl.ds(pl.multiple_of(start, 256), 256)
            part = jnp.dot(ht[rows, :], gbuf[t % 3], preferred_element_type=F32)
            for j in range(WORDS // QB):
                one, unit_one = quantize(part[:, 2 * j * QB : (2 * j + 1) * QB])
                two, unit_two = quantize(part[:, (2 * j + 1) * QB : (2 * j + 2) * QB])
                scale = jnp.broadcast_to(jnp.minimum(unit_one, unit_two) * 2.0**23, (256, QB))
                one = one * 4096.0
                at = slice(first, first + 256), slice(j * QB, (j + 1) * QB)
                if mine:
                    for i, value in enumerate((one, two, scale)):
                        own[t % 2, i, *at] = value
                else:
                    qsend[t % 4, *at] = pack(one, two, scale)

    def compute_theirs(t):
        @pl.when(t + 2 < chunks)
        def _():
            load(t + 2).start()

        load(t).wait()

        @pl.when(t >= 4)
        def _():
            core_copy(t - 4).wait_send()

        compute(t, False)

        @pl.when(t == 0)
        def _():
            pl.semaphore_wait(barrier, len(peers))

        core_copy(t).start()

    def compute_mine(t):
        compute(t, True)

    def stage1(t):
        k = t % SLOTS
        core_copy(t).wait_recv()

        def pair(first, index, count):
            rows = pl.ds(pl.multiple_of(first + index * count, 8), count)
            return join(unpack(qrecv[t, rows]), tuple(own[t % 2, i, rows] for i in range(3)))

        xas[k] = pack(*pair(0, other, NY * ROWS_A))
        xa_copy(t).start()
        ahead, behind = turn(t, 1)
        y1bs[k] = pack(*pair(SEC_A, far, NX * ROWS_B))
        y1_copy(t, 1).start()
        y2bs[k, 0] = pack(*pair(SEC_A, behind, NX * ROWS_B))
        y2_copy(t, 1, 0).start()
        for i, value in enumerate(pair(0, x, NY * ROWS_A)):
            sa[k, i] = value
        for j, row in enumerate((ahead, y)):
            for i, value in enumerate(pair(SEC_A, row, NX * ROWS_B)):
                sb[k, j, i] = value

    def stage2(t):
        k = t % SLOTS
        xa_copy(t).wait()

        def pair(row):
            rows = rows_of(row, ROWS_A)
            return join(unpack(xa[t, rows]), tuple(sa[k, i, rows] for i in range(3)))

        ahead, behind = turn(t, 0)
        y1as[k] = pack(*pair(far))
        y1_copy(t, 0).start()
        y2as[k, 0] = pack(*pair(behind))
        y2_copy(t, 0, 0).start()
        for row in (ahead, y):
            for i, value in enumerate(pair(row)):
                sa[k, i, rows_of(row, ROWS_A)] = value
        y1_copy(t, 1).wait()
        y2bs[k, 1] = pack(*join(unpack(y1b[t]), tuple(sb[k, 0, i] for i in range(3))))
        y2_copy(t, 1, 1).start()

    def stage3(t):
        k = t % SLOTS
        y1_copy(t, 0).wait()
        rows = rows_of(turn(t, 0)[0], ROWS_A)
        y2as[k, 1] = pack(*join(unpack(y1a[t]), tuple(sa[k, i, rows] for i in range(3))))
        y2_copy(t, 0, 1).start()
        y2_copy(t, 1, 0).wait()
        y2_copy(t, 1, 1).wait()

        def pair(index):
            rows = rows_of(index, ROWS_B)
            held = tuple(sb[k, 1, i, rows] for i in range(3))
            return join(join(unpack(y2b[t, 0, rows]), unpack(y2b[t, 1, rows])), held)

        xbs[k] = pack(*pair(other))
        xb_copy(t).start()
        for i, value in enumerate(pair(x)[:2]):
            sb[k, 0, i, :ROWS_B] = value

    def stage4(t):
        k = t % SLOTS
        y2_copy(t, 0, 0).wait()
        y2_copy(t, 0, 1).wait()
        rows = rows_of(y, ROWS_A)
        left, right = unpack(y2a[t, 0]), unpack(y2a[t, 1])
        sum_a = [sa[k, i, rows] + left[i] + right[i] for i in range(2)]
        xb_copy(t).wait()
        last = unpack(xb[t])
        sum_b = [sb[k, 0, i, :ROWS_B] + last[i] for i in range(2)]
        group = (t // 2) % SLOTS
        for total, node, count in ((sum_a, 0, NODE_A), (sum_b, NODE_A, NODE_B)):
            for j in range(WORDS // QB):
                cut = slice(j * QB, (j + 1) * QB)
                pieces = [
                    quantize(total[0][:, cut] * (1.0 / 4096.0))[0].reshape(count, 8, QB),
                    quantize(total[1][:, cut])[0].reshape(count, 8, QB),
                ]
                ns[group, node : node + count, t % 2, :, cut] = jnp.concatenate(pieces, axis=1).astype(BF16)

        @pl.when(t % 2 == 1)
        def _():
            for j in range(1, N_NODE):
                node_send(t // 2, j).start()

    def stage5(t):
        @pl.when(t % 2 == 1)
        def _():
            group = t // 2
            node_all(group).wait()
            for part in range(2):
                total = ns[group % SLOTS, me, part].astype(F32)
                for j in range(1, N_NODE):
                    total = total + nr[group, (me + j) % N_NODE, part].astype(F32)
                for j in range(SPAN // QB):
                    start = (2 * group + part) * SPAN + j * QB
                    cols = pl.ds(pl.multiple_of(start, QB), QB)
                    row, lane = 8 * (j % 2), j // 2 * QB
                    out[:, cols] = total[row : row + 8, lane : lane + QB]

    rounds = (near, ring, [{"node": (me + k) % N_NODE} for k in range(1, N_NODE)])
    places = (0, 3, 6)

    def flag_copies(index):
        return [
            remote(
                fsend.at[index], frecv.at[places[index] + i],
                flag_s.at[places[index] + i], flag_r.at[places[index] + i], device,
            )
            for i, device in enumerate(rounds[index])
        ]

    def flag_round(index):
        if index == 0:
            value = functools.reduce(jnp.maximum, [flag[:, j * QB : (j + 1) * QB] for j in range(WORDS // QB)])
        else:
            value = fsend[index - 1]
            for i, copy in enumerate(flag_copies(index - 1)):
                copy.wait()
                value = jnp.maximum(value, frecv[places[index - 1] + i])
        if index == len(rounds):
            flag_out[0, 0] = jnp.max(value)
            return
        fsend[index] = value
        for copy in flag_copies(index):
            copy.start()

    def step(t, carry):
        def run(body, lag):
            pl.when((t >= lag) & (t < chunks + lag))(lambda: body(t - lag))

        run(compute_theirs, 0)
        run(stage1, PACKED_LAG[1])
        run(stage3, PACKED_LAG[3])
        for index in range(len(rounds)):
            pl.when(t == chunks - 1 + PACKED_LAG[3] + index)(functools.partial(flag_round, index))
        run(compute_mine, 0)
        run(stage2, PACKED_LAG[2])
        run(stage4, PACKED_LAG[4])
        run(stage5, PACKED_LAG[5])
        return carry

    lax.fori_loop(0, chunks + PACKED_LAG[-1], step, 0)
    flag_round(len(rounds))
    for t in range(chunks - 4, chunks):
        core_copy(t).wait_send()


def arrange(hidden_acts):
    tokens = hidden_acts.shape[0]
    blocked = hidden_acts.T.reshape(N_NODE, NY, NX, NC, 8, tokens)
    first = blocked[:NODE_A].transpose(3, 2, 1, 0, 4, 5).reshape(NC, SEC_A, tokens)
    second = blocked[NODE_A:].transpose(3, 1, 2, 0, 4, 5).reshape(NC, SEC_B, tokens)
    return jnp.concatenate([first, second], axis=1).reshape(NC * HALF, tokens)


def call(body, chunks, collective_id, ht, grad_out, has_flag, scratch):
    tokens, width = grad_out.shape
    vmem_spec = pl.BlockSpec(memory_space=pltpu.VMEM)
    out_shape, out_specs = [jax.ShapeDtypeStruct((8, width), F32)], [vmem_spec]
    if has_flag:
        out_shape.append(jax.ShapeDtypeStruct((1, 1), F32))
        out_specs.append(pl.BlockSpec(memory_space=pltpu.SMEM))
    return pl.pallas_call(
        functools.partial(body, chunks),
        out_shape=out_shape,
        in_specs=[vmem_spec, pl.BlockSpec(memory_space=pl.ANY)],
        out_specs=out_specs,
        scratch_shapes=scratch,
        compiler_params=pltpu.CompilerParams(
            collective_id=collective_id, has_side_effects=True, vmem_limit_bytes=58 * 2**20
        ),
        cost_estimate=pl.CostEstimate(
            flops=2 * tokens * NC * HALF * width, bytes_accessed=2 * tokens * (width + NC * HALF), transcendentals=0
        ),
    )(ht, grad_out)


def wide(ht, grad_out):
    tokens, width = grad_out.shape
    chunks, half = width // COLS, COLS // 2
    vmem, dma = pltpu.VMEM, pltpu.SemaphoreType.DMA
    scratch = [
        vmem((3, tokens, COLS), BF16),
        vmem((4, HALF, COLS), BF16),
        vmem((chunks, HALF, COLS), BF16),
        vmem((chunks, NX, NY, ROWS_A, COLS), F32),
        vmem((chunks, NY, NX, ROWS_B, COLS), F32),
        vmem((chunks, NY, ROWS_A, COLS), F32),
        vmem((chunks, 2, ROWS_A, half), F32),
        vmem((chunks, 2, ROWS_A, COLS), F32),
        vmem((chunks, 2, NX, ROWS_B, half), F32),
        vmem((chunks, 2, NX, ROWS_B, COLS), F32),
        vmem((chunks, ROWS_B, COLS), F32),
        vmem((chunks, N_NODE, 16, half), BF16),
        vmem((chunks, N_NODE, 16, half), BF16),
        dma((3,)),
        *[dma((SLOTS,))] * 2,
        *[dma((SLOTS, 2))] * 2,
        *[dma((SLOTS, 2, 2))] * 4,
        *[dma((SLOTS, N_NODE))] * 2,
    ]
    return call(wide_kernel, chunks, 1, ht, grad_out, False, scratch)[0]


def packed(ht, grad_out):
    tokens, width = grad_out.shape
    chunks = width // SPAN
    vmem, dma = pltpu.VMEM, pltpu.SemaphoreType.DMA
    sizes = [(NY * ROWS_A,), (ROWS_A,), (2, ROWS_A), (NX * ROWS_B,), (2, NX * ROWS_B), (ROWS_B,)]
    scratch = [
        vmem((3, tokens, SPAN), BF16),
        vmem((4, HALF, WORDS), F32),
        vmem((chunks, HALF, WORDS), F32),
        vmem((2, 3, HALF, WORDS), F32),
        vmem((SLOTS, 3, NY * ROWS_A, WORDS), F32),
        vmem((SLOTS, 2, 3, NX * ROWS_B, WORDS), F32),
        *[vmem((SLOTS, *size, WORDS), F32) for size in sizes],
        *[vmem((chunks, *size, WORDS), F32) for size in sizes],
        vmem((SLOTS, N_NODE, 2, 16, WORDS), BF16),
        vmem((chunks // 2, N_NODE, 2, 16, WORDS), BF16),
        vmem((8, WORDS), F32),
        vmem((3, 8, QB), F32),
        vmem((13, 8, QB), F32),
        dma((3,)),
        *[dma((SLOTS,))] * 2,
        *[dma((SLOTS, 2))] * 4,
        *[dma((SLOTS, 2, 2))] * 2,
        *[dma((SLOTS,))] * 2,
        *[dma((13,))] * 2,
    ]
    out, flag = call(packed_kernel, chunks, 0, ht, grad_out, True, scratch)
    return out, flag[0, 0] >= 0.0


def per_device(hidden_acts, grad_out):
    ht = arrange(hidden_acts)
    out, misfit = packed(ht, grad_out)
    return lax.cond(misfit, lambda: wide(ht, grad_out), lambda: out)


def solution(mesh):
    return jax.shard_map(
        per_device,
        mesh=mesh,
        in_specs=(P(("node", "local"), None), P(("node", "local"), None)),
        out_specs=P(("node", "local"), None),
        check_vma=False,
    )
```

```python
import functools

import jax
import jax.numpy as jnp
from jax import lax
from jax.experimental import pallas as pl
from jax.experimental.pallas import tpu as pltpu
from jax.sharding import PartitionSpec as P

QB = 128
NY, NX, NC = 4, 2, 2
N_NODE = 8
NODE_A = 3
NODE_B = N_NODE - NODE_A
ROWS_A, ROWS_B = 8 * NODE_A, 8 * NODE_B
SEC_A, SEC_B = NX * NY * ROWS_A, NX * NY * ROWS_B
HALF = SEC_A + SEC_B
COLS = 256
SPAN = 512
WORDS = SPAN // 2
SLOTS = 8
PACKED_LAG = (0, 1, 2, 4, 5, 7, 8)
NZ, NX_HI = 4, 2
LAG = (1, 3, 5, 7, 9)
MESH = pl.DeviceIdType.MESH
F32, BF16 = jnp.float32, jnp.bfloat16


def block_levels(values):
    peak = jnp.max(jnp.abs(values), axis=-1, keepdims=True)
    scaled = peak * (2.0**23 + 1.0)
    power = jnp.maximum(scaled - scaled * (1.0 - 2.0**-24), 2.0**-64)
    levels = jnp.floor(values * (64.0 / power) + 0.5)
    return jnp.minimum(jnp.maximum(levels, -127.0), 127.0), power


def quantize(values):
    levels, power = block_levels(values)
    return levels * (power * (1.0 / 64.0))


def wide_kernel(
    chunks, ht, grad, out,
    gbuf, qsend, qrecv, sa, sb, xa, y1a, y2a, y1b, y2b, xb, ns, nr,
    gsem, core_s, core_r, x_s, x_r, y1_s, y1_r, y2_s, y2_r, node_s, node_r,
):
    me = lax.axis_index("node")
    loc = lax.axis_index("local")
    c, x, y = loc % NC, (loc // NC) % NX, loc // (NC * NX)
    up, down, far = (y + 1) % NY, (y + NY - 1) % NY, (y + 2) % NY
    sibling = {"local": loc + 1 - 2 * c}
    across = {"local": loc + NC * (1 - 2 * x)}
    above = {"local": (up * NX + x) * NC + c}
    below = {"local": (down * NX + x) * NC + c}
    other = 1 - x
    half = COLS // 2

    def remote(src, dst, s, r, device):
        return pltpu.make_async_remote_copy(
            src_ref=src, dst_ref=dst, send_sem=s, recv_sem=r, device_id=device, device_id_type=MESH
        )

    def load(t):
        cols = pl.ds(pl.multiple_of(t * COLS, COLS), COLS)
        return pltpu.make_async_copy(grad.at[:, cols], gbuf.at[t % 3], gsem.at[t % 3])

    def core_copy(t):
        return remote(qsend.at[t % 4], qrecv.at[t], core_s.at[t % SLOTS], core_r.at[t % SLOTS], sibling)

    def x_copies(t):
        k = t % SLOTS
        return (
            remote(sa.at[t, other], xa.at[t], x_s.at[k, 0], x_r.at[k, 0], across),
            remote(sb.at[t, y, other], xb.at[t], x_s.at[k, 1], x_r.at[k, 1], across),
        )

    def y1_copies(t):
        k = t % SLOTS
        made = []
        for i, (src, dst) in enumerate(((sa.at[t, x, far], y1a), (sb.at[t, far], y1b))):
            for d, device in enumerate((above, below)):
                made.append(
                    remote(
                        src.at[..., pl.ds(d * half, half)], dst.at[t, d],
                        y1_s.at[k, i, d], y1_r.at[k, i, d], device,
                    )
                )
        return made[:2], made[2:]

    def y2_copies(t):
        k = t % SLOTS
        made = []
        for i in range(2):
            for d, (row, device) in enumerate(((up, above), (down, below))):
                src = (sa.at[t, x, row], sb.at[t, row])[i]
                made.append(
                    remote(src, (y2a, y2b)[i].at[t, d], y2_s.at[k, i, d], y2_r.at[k, i, d], device)
                )
        return made[:2], made[2:]

    def node_send(t, k):
        to = (me + k) % N_NODE
        return remote(
            ns.at[t, to], nr.at[t, me], node_s.at[t % SLOTS, k], node_r.at[t % SLOTS, k], {"node": to}
        )

    def node_recv(t, k):
        source = (me + N_NODE - k) % N_NODE
        return remote(
            ns.at[t, source], nr.at[t, source],
            node_s.at[t % SLOTS, k], node_r.at[t % SLOTS, k], {"node": source},
        )

    def start(copies):
        for copy in copies:
            copy.start()

    def wait(copies):
        for copy in copies:
            copy.wait()

    barrier = pltpu.get_barrier_semaphore()
    peers = [sibling, across, above, below] + [{"node": (me + k) % N_NODE} for k in range(1, N_NODE)]
    load(0).start()
    load(1).start()
    for peer in peers:
        pl.semaphore_signal(barrier, inc=1, device_id=peer, device_id_type=MESH)
    pl.semaphore_wait(barrier, len(peers))

    def compute(t):
        @pl.when(t + 2 < chunks)
        def _():
            load(t + 2).start()

        load(t).wait()

        @pl.when(t >= 4)
        def _():
            core_copy(t - 4).wait_send()

        block = gbuf.at[t % 3]
        for first, count in ((0, 256), (256, 256)):
            rows = pl.ds(pl.multiple_of((1 - c) * HALF + first, 64), count)
            part = jnp.dot(ht[rows, :], block[...], preferred_element_type=F32)
            for j in range(COLS // QB):
                cut = slice(j * QB, (j + 1) * QB)
                qsend[t % 4, first : first + count, cut] = quantize(part[:, cut]).astype(BF16)
        core_copy(t).start()
        for first, count, dst, shape in (
            (0, SEC_A, sa, (NX, NY, ROWS_A, QB)),
            (SEC_A, SEC_B, sb, (NY, NX, ROWS_B, QB)),
        ):
            rows = pl.ds(pl.multiple_of(c * HALF + first, 64), count)
            part = jnp.dot(ht[rows, :], block[...], preferred_element_type=F32)
            for j in range(COLS // QB):
                cut = slice(j * QB, (j + 1) * QB)
                dst[t, :, :, :, cut] = quantize(part[:, cut]).reshape(shape)

    def stage1(t):
        core_copy(t).wait_recv()
        sa[t] = sa[t] + qrecv[t, :SEC_A].astype(F32).reshape(NX, NY, ROWS_A, COLS)
        x_copies(t)[0].start()
        sb[t] = sb[t] + qrecv[t, SEC_A:].astype(F32).reshape(NY, NX, ROWS_B, COLS)
        start(y1_copies(t)[1])

    def stage2(t):
        x_copies(t)[0].wait()
        sa[t, x] = sa[t, x] + xa[t]
        start(y1_copies(t)[0])
        wait(y1_copies(t)[1])
        sb[t, up, :, :, :half] = sb[t, up, :, :, :half] + y1b[t, 0]
        sb[t, down, :, :, half:] = sb[t, down, :, :, half:] + y1b[t, 1]
        start(y2_copies(t)[1])

    def stage3(t):
        wait(y1_copies(t)[0])
        sa[t, x, up, :, :half] = sa[t, x, up, :, :half] + y1a[t, 0]
        sa[t, x, down, :, half:] = sa[t, x, down, :, half:] + y1a[t, 1]
        start(y2_copies(t)[0])
        wait(y2_copies(t)[1])
        sb[t, y] = sb[t, y] + y2b[t, 0] + y2b[t, 1]
        x_copies(t)[1].start()

    def stage4(t):
        wait(y2_copies(t)[0])
        sum_a = sa[t, x, y] + y2a[t, 0] + y2a[t, 1]
        x_copies(t)[1].wait()
        sum_b = sb[t, y, x] + xb[t]
        for total, node, count in ((sum_a, 0, NODE_A), (sum_b, NODE_A, NODE_B)):
            pieces = [
                quantize(total[:, j * QB : (j + 1) * QB]).reshape(count, 8, QB) for j in range(COLS // QB)
            ]
            ns[t, node : node + count] = jnp.concatenate(pieces, axis=1).astype(BF16)
        for k in range(1, N_NODE):
            node_send(t, k).start()

    def stage5(t):
        total = ns[t, me].astype(F32)
        for k in range(1, N_NODE):
            node_send(t, k).wait_send()
            node_recv(t, k).wait_recv()
            total = total + nr[t, (me + N_NODE - k) % N_NODE].astype(F32)
        for j in range(COLS // QB):
            cols = pl.ds(pl.multiple_of(t * COLS + j * QB, QB), QB)
            out[:, cols] = total[8 * j : 8 * j + 8]

    def step(t, carry):
        pl.when(t < chunks)(lambda: compute(t))
        for lag, stage in zip(LAG, (stage1, stage2, stage3, stage4, stage5)):
            pl.when((t >= lag) & (t < chunks + lag))(functools.partial(stage, t - lag))
        return carry

    lax.fori_loop(0, chunks + LAG[-1], step, 0)
    for t in range(chunks - 4, chunks):
        core_copy(t).wait_send()


def split_power(words):
    scaled = words * (2.0**23 + 1.0)
    return scaled - scaled * (1.0 - 2.0**-24)


def unpack(words):
    signed = split_power(words)
    both = words - signed
    scale = jnp.abs(signed)
    magic = scale * 6144.0
    first = (both + magic) - magic
    return first, both - first, scale


def packed_kernel(
    chunks, ht, grad, out, flag_out,
    gbuf, qsend, qrecv, own, sa, sb,
    xas, y1as, y2as, y1bs, y2bs, xbs, xa, y1a, y2a, y1b, y2b, xb, ns, nr, held, hs, hr, direct, flag, fsend, frecv,
    gsem, core_s, core_r, x_s, x_r, y1_s, y1_r, y2_s, y2_r, node_s, node_r, half_s, half_r, direct_s, direct_r, flag_s, flag_r,
):
    me = lax.axis_index("node")
    loc = lax.axis_index("local")
    c, x, y = lax.rem(loc, NC), lax.rem(lax.div(loc, NC), NX), lax.div(loc, NC * NX)
    far, sides = lax.rem(y + 2, NY), (lax.rem(y + 1, NY), lax.rem(y + 3, NY))
    other = 1 - x
    x_hi, z = lax.div(me, NZ), lax.rem(me, NZ)
    relayed = chunks // 4
    opposite = {"node": me + NZ * (1 - 2 * x_hi)}

    def at_y(row):
        return {"local": (row * NX + x) * NC + c}

    sibling = {"local": loc + 1 - 2 * c}
    across = {"local": loc + NC * (1 - 2 * x)}
    ring = [at_y(row) for row in sides]
    mates = [
        {"local": (lax.rem(y + j // 4, NY) * NX + lax.rem(x + j // 2 % 2, NX)) * NC + lax.rem(c + j % 2, NC)}
        for j in range(1, NY * NX * NC)
    ]
    nodes = [{"node": lax.rem(x_hi + j // NZ, NX_HI) * NZ + lax.rem(z + j % NZ, NZ)} for j in range(1, N_NODE)]

    def remote(src, dst, s, r, device):
        return pltpu.make_async_remote_copy(
            src_ref=src, dst_ref=dst, send_sem=s, recv_sem=r, device_id=device, device_id_type=MESH
        )

    def load(t):
        cols = pl.ds(pl.multiple_of(t * SPAN, SPAN), SPAN)
        return pltpu.make_async_copy(grad.at[:, cols], gbuf.at[lax.rem(t, 3)], gsem.at[lax.rem(t, 3)])

    def turn(t):
        odd = lax.rem(t, 2)
        return lax.rem(y + 1 + 2 * odd, NY), lax.rem(y + 3 - 2 * odd, NY)

    def pack(first, second, scale):
        both = first + second
        excess = jnp.maximum(jnp.abs(both), jnp.abs(second) * 4096.0) - scale
        width = scale.shape[-1]
        flag[:, :width] = jnp.maximum(flag[:, :width], jnp.max(excess.reshape(-1, 8, width), axis=0))
        return both + jnp.where(both < 0.0, -scale, scale)

    def join(left, right):
        return left[0] + right[0], left[1] + right[1], jnp.minimum(left[2], right[2])

    def rows_of(index, count):
        return pl.ds(pl.multiple_of(index * count, 8), count)

    barrier = pltpu.get_barrier_semaphore()
    peers = mates + nodes
    load(0).start()
    load(1).start()
    for peer in peers:
        pl.semaphore_signal(barrier, inc=1, device_id=peer, device_id_type=MESH)
    flag[...] = jnp.full((8, WORDS), -1.0, F32)

    def core_copy(t):
        k = lax.rem(t, SLOTS)
        return remote(qsend.at[lax.rem(t, 2)], qrecv.at[t], core_s.at[k], core_r.at[k], sibling)

    def xa_copy(t):
        k = lax.rem(t, SLOTS)
        return remote(xas.at[k], xa.at[t], x_s.at[k, 0], x_r.at[k, 0], across)

    def xb_copy(t):
        k = lax.rem(t, SLOTS)
        return remote(xbs.at[k], xb.at[t], x_s.at[k, 1], x_r.at[k, 1], across)

    def y1a_copy(t):
        k = lax.rem(t, SLOTS)
        return remote(y1as.at[k], y1a.at[t], y1_s.at[k, 2], y1_r.at[k, 2], at_y(turn(t)[0]))

    def y1b_copy(t, d):
        k = lax.rem(t, SLOTS)
        return remote(y1bs.at[k, d], y1b.at[t, d], y1_s.at[k, d], y1_r.at[k, d], ring[d])

    def y2a_copy(t, late):
        k = lax.rem(t, SLOTS)
        return remote(
            y2as.at[k, late], y2a.at[t, late], y2_s.at[k, 2, late], y2_r.at[k, 2, late], at_y(turn(t)[1 - late])
        )

    def y2b_copy(t, d, late):
        k = lax.rem(t, SLOTS)
        return remote(
            y2bs.at[k, d, late], y2b.at[t, d, late], y2_s.at[k, d, late], y2_r.at[k, d, late], ring[d]
        )

    def z_copies(group):
        k = lax.rem(group, SLOTS)
        return [
            remote(
                ns.at[k, lax.rem(z + j, NZ)], nr.at[group, z],
                node_s.at[k], node_r.at[k], {"node": x_hi * NZ + lax.rem(z + j, NZ)},
            )
            for j in range(1, NZ)
        ]

    def z_all(group):
        k, count = lax.rem(group, SLOTS), pl.ds(0, NZ - 1)
        return remote(
            ns.at[k, count], nr.at[group, count],
            node_s.at[k], node_r.at[k], opposite,
        )

    def direct_copies(group):
        k, g = lax.rem(group, SLOTS), group - relayed
        return [
            remote(
                ns.at[k, lax.rem(z + j % NZ, NZ), lax.rem(x_hi + j // NZ, NX_HI)], direct.at[g, j],
                direct_s.at[g], direct_r.at[g],
                {"node": lax.rem(x_hi + j // NZ, NX_HI) * NZ + lax.rem(z + j % NZ, NZ)},
            )
            for j in range(1, N_NODE)
        ]

    def half_copy(group):
        k = lax.rem(group, SLOTS)
        return remote(hs.at[k], hr.at[group], half_s.at[k], half_r.at[k], opposite)

    def compute(t, mine):
        for first in range(0, HALF, 128):
            start = (c if mine else 1 - c) * HALF + first
            rows = pl.ds(pl.multiple_of(start, 128), 128)
            part = jnp.dot(ht[rows, :], gbuf[lax.rem(t, 3)], preferred_element_type=F32)
            for j in range(WORDS // QB):
                one, power_one = block_levels(part[:, 2 * j * QB : (2 * j + 1) * QB])
                two, power_two = block_levels(part[:, (2 * j + 1) * QB : (2 * j + 2) * QB])
                one, two = one * (power_one * 64.0), two * (power_two * (1.0 / 64.0))
                least = jnp.minimum(power_one, power_two)
                scale = jnp.broadcast_to(least * 2.0**17, (128, QB))
                at = slice(first, first + 128), slice(j * QB, (j + 1) * QB)
                if mine:
                    for i, value in enumerate((one, two, scale)):
                        own[lax.rem(t, 2), i, *at] = value
                else:
                    excess = jnp.maximum(power_one, power_two) - least * 32.0
                    flag[:, :QB] = jnp.maximum(flag[:, :QB], jnp.max(excess.reshape(-1, 8, 1), axis=0))
                    both = one + two
                    qsend[lax.rem(t, 2), *at] = both + jnp.where(both < 0.0, -scale, scale)

    def compute_theirs(t):
        pl.when(t + 2 < chunks)(lambda: load(t + 2).start())
        load(t).wait()
        compute(t, False)

        @pl.when(t == 0)
        def _():
            pl.semaphore_wait(barrier, len(peers))

        core_copy(t).start()

    def compute_mine(t):
        compute(t, True)

    def stage1(t):
        k = lax.rem(t, SLOTS)
        core_copy(t).wait()

        def pair(first, index, count):
            rows = pl.ds(pl.multiple_of(first + index * count, 8), count)
            return join(unpack(qrecv[t, rows]), tuple(own[lax.rem(t, 2), i, rows] for i in range(3)))

        for d in range(2):
            y1bs[k, d] = pack(*pair(SEC_A, far * NX + d, ROWS_B))
            y1b_copy(t, d).start()
        xas[k] = pack(*pair(0, other, NY * ROWS_A))
        xa_copy(t).start()
        for d in range(2):
            y2bs[k, d, 0] = pack(*pair(SEC_A, sides[d] * NX + 1 - d, ROWS_B))
            y2b_copy(t, d, 0).start()
        for i, value in enumerate(pair(0, x, NY * ROWS_A)):
            sa[k, i] = value
        for j, index in enumerate((sides[0] * NX, sides[1] * NX + 1, y * NX, y * NX + 1)):
            for i, value in enumerate(pair(SEC_A, index, ROWS_B)):
                sb[k, j, i] = value

    def stage2(t):
        k = lax.rem(t, SLOTS)
        for d in range(2):
            y1b_copy(t, d).wait()
            y2bs[k, d, 1] = pack(*join(unpack(y1b[t, d]), tuple(sb[k, d, i] for i in range(3))))
            y2b_copy(t, d, 1).start()
        xa_copy(t).wait()

        def pair(row):
            rows = rows_of(row, ROWS_A)
            return join(unpack(xa[t, rows]), tuple(sa[k, i, rows] for i in range(3)))

        ahead, behind = turn(t)
        y1as[k] = pack(*pair(far))
        y1a_copy(t).start()
        y2as[k, 0] = pack(*pair(behind))
        y2a_copy(t, 0).start()
        for row in (ahead, y):
            for i, value in enumerate(pair(row)):
                sa[k, i, rows_of(row, ROWS_A)] = value

    def stage3(t):
        k = lax.rem(t, SLOTS)
        y1a_copy(t).wait()
        rows = rows_of(turn(t)[0], ROWS_A)
        y2as[k, 1] = pack(*join(unpack(y1a[t]), tuple(sa[k, i, rows] for i in range(3))))
        y2a_copy(t, 1).start()
        for d in range(2):
            for late in range(2):
                y2b_copy(t, d, late).wait()

        def pair(index):
            mine = tuple(sb[k, 2 + index, i] for i in range(3))
            return join(join(unpack(y2b[t, 0, 1 - index]), unpack(y2b[t, 1, index])), mine)

        xbs[k] = pack(*pair(other))
        xb_copy(t).start()
        for i, value in enumerate(pair(x)[:2]):
            sb[k, 0, i] = value

    def stage4(t):
        k = lax.rem(t, SLOTS)
        y2a_copy(t, 0).wait()
        y2a_copy(t, 1).wait()
        rows = rows_of(y, ROWS_A)
        left, right = unpack(y2a[t, 0]), unpack(y2a[t, 1])
        sum_a = [sa[k, i, rows] + left[i] + right[i] for i in range(2)]
        xb_copy(t).wait()
        last = unpack(xb[t])
        sum_b = [sb[k, 0, i] + last[i] for i in range(2)]
        group = lax.rem(lax.div(t, 2), SLOTS)
        for j in range(WORDS // QB):
            cut = slice(j * QB, (j + 1) * QB)
            for total, node, count in ((sum_a, 0, NODE_A), (sum_b, NODE_A, NODE_B)):
                pieces = [
                    quantize(total[0][:, cut] * (1.0 / 4096.0)).reshape(count, 8, QB),
                    quantize(total[1][:, cut]).reshape(count, 8, QB),
                ]
                blocks = jnp.concatenate(pieces, axis=1).astype(BF16)
                for n in range(count):
                    ns[group, (node + n) % NZ, (node + n) // NZ, lax.rem(t, 2), :, cut] = blocks[n]

        @pl.when((lax.rem(t, 2) == 1) & (t < 2 * relayed))
        def _():
            for copy in z_copies(lax.div(t, 2)):
                copy.start()

        @pl.when((lax.rem(t, 2) == 1) & (t >= 2 * relayed))
        def _():
            for copy in direct_copies(lax.div(t, 2)):
                copy.start()

    def stage5(t):
        group = lax.div(t, 2)
        k = lax.rem(group, SLOTS)
        z_all(group).wait()

        def total(index):
            value = ns[k, z, index, :].astype(F32)
            for j in range(1, NZ):
                value = value + nr[group, lax.rem(z + j, NZ), index, :].astype(F32)
            return value

        hs[k, :] = total(1 - x_hi)
        half_copy(group).start()
        held[k, :] = total(x_hi)

    def stage6(t):
        group = lax.div(t, 2)
        k = lax.rem(group, SLOTS)
        half_copy(group).wait()
        for part in range(2):
            store(t - 1 + part, held[k, part] + hr[group, part])

    def store(t, total):
        for j in range(SPAN // QB):
            cols = pl.ds(pl.multiple_of(t * SPAN + j * QB, QB), QB)
            row, lane = 8 * (j % 2), j // 2 * QB
            out[:, cols] = total[row : row + 8, lane : lane + QB]

    def finish(group):
        g, count = group - relayed, pl.ds(1, N_NODE - 1)
        remote(direct.at[g, count], direct.at[g, count], direct_s.at[g], direct_r.at[g], opposite).wait()
        total = ns[group % SLOTS, z, x_hi].astype(F32)
        for j in range(1, N_NODE):
            total = total + direct[g, j].astype(F32)
        for part in range(2):
            store(2 * group + part, total[part])

    rounds = (mates, nodes)
    places = (0, len(mates))

    def flag_copies(index):
        return [
            remote(
                fsend.at[index], frecv.at[places[index] + i],
                flag_s.at[places[index] + i], flag_r.at[places[index] + i], device,
            )
            for i, device in enumerate(rounds[index])
        ]

    def flag_round(index):
        if index == 0:
            value = functools.reduce(jnp.maximum, [flag[:, j * QB : (j + 1) * QB] for j in range(WORDS // QB)])
        else:
            value = fsend[index - 1]
            for i, copy in enumerate(flag_copies(index - 1)):
                copy.wait()
                value = jnp.maximum(value, frecv[places[index - 1] + i])
        if index == len(rounds):
            flag_out[0, 0] = jnp.max(value)
            return
        fsend[index] = value
        for copy in flag_copies(index):
            copy.start()

    def step(t, carry):
        def run(body, stage, end=chunks, odd=False):
            now = t - PACKED_LAG[stage]
            inside = (now >= 0) & (now < end)
            if odd:
                inside = inside & (lax.rem(t, 2) == (PACKED_LAG[stage] + 1) % 2)
            pl.when(inside)(lambda: body(now))

        run(compute_theirs, 0)
        pl.when((t >= 2) & (t <= chunks))(lambda: stage1(t - 1))
        run(stage3, 3)
        pl.when(t == chunks - 1 + PACKED_LAG[3])(lambda: flag_round(0))
        run(compute_mine, 0)
        pl.when(t == 0)(lambda: stage1(t))
        run(stage2, 2)
        run(stage4, 4)
        pl.when(t == chunks - 1 + PACKED_LAG[4])(lambda: flag_round(1))
        run(stage5, 5, 2 * relayed, True)
        run(stage6, 6, 2 * relayed, True)
        return carry

    lax.fori_loop(0, chunks + PACKED_LAG[4], step, 0)
    for group in range(relayed, chunks // 2):
        finish(group)
    flag_round(2)


def arrange(hidden_acts):
    tokens = hidden_acts.shape[0]
    blocked = hidden_acts.T.reshape(N_NODE, NY, NX, NC, 8, tokens)
    first = blocked[:NODE_A].transpose(3, 2, 1, 0, 4, 5).reshape(NC, SEC_A, tokens)
    second = blocked[NODE_A:].transpose(3, 1, 2, 0, 4, 5).reshape(NC, SEC_B, tokens)
    return jnp.concatenate([first, second], axis=1).reshape(NC * HALF, tokens)


def call(body, chunks, collective_id, ht, grad_out, has_flag, scratch):
    tokens, width = grad_out.shape
    vmem_spec = pl.BlockSpec(memory_space=pltpu.VMEM)
    out_shape, out_specs = [jax.ShapeDtypeStruct((8, width), F32)], [vmem_spec]
    if has_flag:
        out_shape.append(jax.ShapeDtypeStruct((1, 1), F32))
        out_specs.append(pl.BlockSpec(memory_space=pltpu.SMEM))
    return pl.pallas_call(
        functools.partial(body, chunks),
        out_shape=out_shape,
        in_specs=[vmem_spec, pl.BlockSpec(memory_space=pl.ANY)],
        out_specs=out_specs,
        scratch_shapes=scratch,
        compiler_params=pltpu.CompilerParams(
            collective_id=collective_id, has_side_effects=True, vmem_limit_bytes=58 * 2**20
        ),
        cost_estimate=pl.CostEstimate(
            flops=2 * tokens * NC * HALF * width, bytes_accessed=2 * tokens * (width + NC * HALF), transcendentals=0
        ),
    )(ht, grad_out)


def wide(ht, grad_out):
    tokens, width = grad_out.shape
    chunks, half = width // COLS, COLS // 2
    vmem, dma = pltpu.VMEM, pltpu.SemaphoreType.DMA
    scratch = [
        vmem((3, tokens, COLS), BF16),
        vmem((4, HALF, COLS), BF16),
        vmem((chunks, HALF, COLS), BF16),
        vmem((chunks, NX, NY, ROWS_A, COLS), F32),
        vmem((chunks, NY, NX, ROWS_B, COLS), F32),
        vmem((chunks, NY, ROWS_A, COLS), F32),
        vmem((chunks, 2, ROWS_A, half), F32),
        vmem((chunks, 2, ROWS_A, COLS), F32),
        vmem((chunks, 2, NX, ROWS_B, half), F32),
        vmem((chunks, 2, NX, ROWS_B, COLS), F32),
        vmem((chunks, ROWS_B, COLS), F32),
        vmem((chunks, N_NODE, 16, half), BF16),
        vmem((chunks, N_NODE, 16, half), BF16),
        dma((3,)),
        *[dma((SLOTS,))] * 2,
        *[dma((SLOTS, 2))] * 2,
        *[dma((SLOTS, 2, 2))] * 4,
        *[dma((SLOTS, N_NODE))] * 2,
    ]
    return call(wide_kernel, chunks, 1, ht, grad_out, False, scratch)[0]


def packed(ht, grad_out):
    tokens, width = grad_out.shape
    chunks = width // SPAN
    vmem, dma = pltpu.VMEM, pltpu.SemaphoreType.DMA
    sizes = [(NY * ROWS_A,), (ROWS_A,), (2, ROWS_A), (2, ROWS_B), (2, 2, ROWS_B), (ROWS_B,)]
    scratch = [
        vmem((3, tokens, SPAN), BF16),
        vmem((2, HALF, WORDS), F32),
        vmem((chunks, HALF, WORDS), F32),
        vmem((2, 3, HALF, WORDS), F32),
        vmem((SLOTS, 3, NY * ROWS_A, WORDS), F32),
        vmem((SLOTS, 4, 3, ROWS_B, WORDS), F32),
        *[vmem((SLOTS, *size, WORDS), F32) for size in sizes],
        *[vmem((chunks, *size, WORDS), F32) for size in sizes],
        vmem((SLOTS, NZ, NX_HI, 2, 16, WORDS), BF16),
        vmem((chunks // 2, NZ, NX_HI, 2, 16, WORDS), BF16),
        vmem((SLOTS, 2, 16, WORDS), F32),
        vmem((SLOTS, 2, 16, WORDS), F32),
        vmem((chunks // 2, 2, 16, WORDS), F32),
        vmem((chunks // 2 - chunks // 4, N_NODE, 2, 16, WORDS), BF16),
        vmem((8, WORDS), F32),
        vmem((2, 8, QB), F32),
        vmem((22, 8, QB), F32),
        dma((3,)),
        *[dma((SLOTS,))] * 2,
        *[dma((SLOTS, 2))] * 2,
        *[dma((SLOTS, 3))] * 2,
        *[dma((SLOTS, 3, 2))] * 2,
        *[dma((SLOTS,))] * 4,
        *[dma((chunks // 2 - chunks // 4,))] * 2,
        *[dma((22,))] * 2,
    ]
    out, flag = call(packed_kernel, chunks, 0, ht, grad_out, True, scratch)
    return out, flag[0, 0] >= 0.0


def per_device(hidden_acts, grad_out):
    ht = arrange(hidden_acts)
    out, misfit = packed(ht, grad_out)
    return lax.cond(misfit, lambda: wide(ht, grad_out), lambda: out)


def solution(mesh):
    return jax.shard_map(
        per_device,
        mesh=mesh,
        in_specs=(P(("node", "local"), None), P(("node", "local"), None)),
        out_specs=P(("node", "local"), None),
        check_vma=False,
    )
```

```python
import functools

import jax
import jax.numpy as jnp
from jax import lax
from jax.experimental import pallas as pl
from jax.experimental.pallas import tpu as pltpu
from jax.sharding import PartitionSpec as P

QB = 128
NY, NX, NC = 4, 2, 2
N_NODE = 8
NODE_A = 3
NODE_B = N_NODE - NODE_A
ROWS_A, ROWS_B = 8 * NODE_A, 8 * NODE_B
SEC_A, SEC_B = NX * NY * ROWS_A, NX * NY * ROWS_B
HALF = SEC_A + SEC_B
COLS = 256
SPAN = 512
WORDS = SPAN // 2
SLOTS = 8
PACKED_LAG = (0, 1, 2, 4, 5, 7, 8)
NZ, NX_HI = 4, 2
LAG = (1, 3, 5, 7, 9)
MESH = pl.DeviceIdType.MESH
F32, BF16 = jnp.float32, jnp.bfloat16


def block_levels(values):
    peak = jnp.max(jnp.abs(values), axis=-1, keepdims=True)
    scaled = peak * (2.0**23 + 1.0)
    power = jnp.maximum(scaled - scaled * (1.0 - 2.0**-24), 2.0**-64)
    levels = jnp.floor(values * (64.0 / power) + 0.5)
    return jnp.minimum(jnp.maximum(levels, -127.0), 127.0), power


def quantize(values):
    levels, power = block_levels(values)
    return levels * (power * (1.0 / 64.0))


def wide_kernel(
    chunks, ht, grad, out,
    gbuf, qsend, qrecv, sa, sb, xa, y1a, y2a, y1b, y2b, xb, ns, nr,
    gsem, core_s, core_r, x_s, x_r, y1_s, y1_r, y2_s, y2_r, node_s, node_r,
):
    me = lax.axis_index("node")
    loc = lax.axis_index("local")
    c, x, y = loc % NC, (loc // NC) % NX, loc // (NC * NX)
    up, down, far = (y + 1) % NY, (y + NY - 1) % NY, (y + 2) % NY
    sibling = {"local": loc + 1 - 2 * c}
    across = {"local": loc + NC * (1 - 2 * x)}
    above = {"local": (up * NX + x) * NC + c}
    below = {"local": (down * NX + x) * NC + c}
    other = 1 - x
    half = COLS // 2

    def remote(src, dst, s, r, device):
        return pltpu.make_async_remote_copy(
            src_ref=src, dst_ref=dst, send_sem=s, recv_sem=r, device_id=device, device_id_type=MESH
        )

    def load(t):
        cols = pl.ds(pl.multiple_of(t * COLS, COLS), COLS)
        return pltpu.make_async_copy(grad.at[:, cols], gbuf.at[t % 3], gsem.at[t % 3])

    def core_copy(t):
        return remote(qsend.at[t % 4], qrecv.at[t], core_s.at[t % SLOTS], core_r.at[t % SLOTS], sibling)

    def x_copies(t):
        k = t % SLOTS
        return (
            remote(sa.at[t, other], xa.at[t], x_s.at[k, 0], x_r.at[k, 0], across),
            remote(sb.at[t, y, other], xb.at[t], x_s.at[k, 1], x_r.at[k, 1], across),
        )

    def y1_copies(t):
        k = t % SLOTS
        made = []
        for i, (src, dst) in enumerate(((sa.at[t, x, far], y1a), (sb.at[t, far], y1b))):
            for d, device in enumerate((above, below)):
                made.append(
                    remote(
                        src.at[..., pl.ds(d * half, half)], dst.at[t, d],
                        y1_s.at[k, i, d], y1_r.at[k, i, d], device,
                    )
                )
        return made[:2], made[2:]

    def y2_copies(t):
        k = t % SLOTS
        made = []
        for i in range(2):
            for d, (row, device) in enumerate(((up, above), (down, below))):
                src = (sa.at[t, x, row], sb.at[t, row])[i]
                made.append(
                    remote(src, (y2a, y2b)[i].at[t, d], y2_s.at[k, i, d], y2_r.at[k, i, d], device)
                )
        return made[:2], made[2:]

    def node_send(t, k):
        to = (me + k) % N_NODE
        return remote(
            ns.at[t, to], nr.at[t, me], node_s.at[t % SLOTS, k], node_r.at[t % SLOTS, k], {"node": to}
        )

    def node_recv(t, k):
        source = (me + N_NODE - k) % N_NODE
        return remote(
            ns.at[t, source], nr.at[t, source],
            node_s.at[t % SLOTS, k], node_r.at[t % SLOTS, k], {"node": source},
        )

    def start(copies):
        for copy in copies:
            copy.start()

    def wait(copies):
        for copy in copies:
            copy.wait()

    barrier = pltpu.get_barrier_semaphore()
    peers = [sibling, across, above, below] + [{"node": (me + k) % N_NODE} for k in range(1, N_NODE)]
    load(0).start()
    load(1).start()
    for peer in peers:
        pl.semaphore_signal(barrier, inc=1, device_id=peer, device_id_type=MESH)
    pl.semaphore_wait(barrier, len(peers))

    def compute(t):
        @pl.when(t + 2 < chunks)
        def _():
            load(t + 2).start()

        load(t).wait()

        @pl.when(t >= 4)
        def _():
            core_copy(t - 4).wait_send()

        block = gbuf.at[t % 3]
        for first, count in ((0, 256), (256, 256)):
            rows = pl.ds(pl.multiple_of((1 - c) * HALF + first, 64), count)
            part = jnp.dot(ht[rows, :], block[...], preferred_element_type=F32)
            for j in range(COLS // QB):
                cut = slice(j * QB, (j + 1) * QB)
                qsend[t % 4, first : first + count, cut] = quantize(part[:, cut]).astype(BF16)
        core_copy(t).start()
        for first, count, dst, shape in (
            (0, SEC_A, sa, (NX, NY, ROWS_A, QB)),
            (SEC_A, SEC_B, sb, (NY, NX, ROWS_B, QB)),
        ):
            rows = pl.ds(pl.multiple_of(c * HALF + first, 64), count)
            part = jnp.dot(ht[rows, :], block[...], preferred_element_type=F32)
            for j in range(COLS // QB):
                cut = slice(j * QB, (j + 1) * QB)
                dst[t, :, :, :, cut] = quantize(part[:, cut]).reshape(shape)

    def stage1(t):
        core_copy(t).wait_recv()
        sa[t] = sa[t] + qrecv[t, :SEC_A].astype(F32).reshape(NX, NY, ROWS_A, COLS)
        x_copies(t)[0].start()
        sb[t] = sb[t] + qrecv[t, SEC_A:].astype(F32).reshape(NY, NX, ROWS_B, COLS)
        start(y1_copies(t)[1])

    def stage2(t):
        x_copies(t)[0].wait()
        sa[t, x] = sa[t, x] + xa[t]
        start(y1_copies(t)[0])
        wait(y1_copies(t)[1])
        sb[t, up, :, :, :half] = sb[t, up, :, :, :half] + y1b[t, 0]
        sb[t, down, :, :, half:] = sb[t, down, :, :, half:] + y1b[t, 1]
        start(y2_copies(t)[1])

    def stage3(t):
        wait(y1_copies(t)[0])
        sa[t, x, up, :, :half] = sa[t, x, up, :, :half] + y1a[t, 0]
        sa[t, x, down, :, half:] = sa[t, x, down, :, half:] + y1a[t, 1]
        start(y2_copies(t)[0])
        wait(y2_copies(t)[1])
        sb[t, y] = sb[t, y] + y2b[t, 0] + y2b[t, 1]
        x_copies(t)[1].start()

    def stage4(t):
        wait(y2_copies(t)[0])
        sum_a = sa[t, x, y] + y2a[t, 0] + y2a[t, 1]
        x_copies(t)[1].wait()
        sum_b = sb[t, y, x] + xb[t]
        for total, node, count in ((sum_a, 0, NODE_A), (sum_b, NODE_A, NODE_B)):
            pieces = [
                quantize(total[:, j * QB : (j + 1) * QB]).reshape(count, 8, QB) for j in range(COLS // QB)
            ]
            ns[t, node : node + count] = jnp.concatenate(pieces, axis=1).astype(BF16)
        for k in range(1, N_NODE):
            node_send(t, k).start()

    def stage5(t):
        total = ns[t, me].astype(F32)
        for k in range(1, N_NODE):
            node_send(t, k).wait_send()
            node_recv(t, k).wait_recv()
            total = total + nr[t, (me + N_NODE - k) % N_NODE].astype(F32)
        for j in range(COLS // QB):
            cols = pl.ds(pl.multiple_of(t * COLS + j * QB, QB), QB)
            out[:, cols] = total[8 * j : 8 * j + 8]

    def step(t, carry):
        pl.when(t < chunks)(lambda: compute(t))
        for lag, stage in zip(LAG, (stage1, stage2, stage3, stage4, stage5)):
            pl.when((t >= lag) & (t < chunks + lag))(functools.partial(stage, t - lag))
        return carry

    lax.fori_loop(0, chunks + LAG[-1], step, 0)
    for t in range(chunks - 4, chunks):
        core_copy(t).wait_send()


def split_power(words):
    scaled = words * (2.0**23 + 1.0)
    return scaled - scaled * (1.0 - 2.0**-24)


def unpack(words):
    signed = split_power(words)
    both = words - signed
    scale = jnp.abs(signed)
    magic = scale * 6144.0
    first = (both + magic) - magic
    return first, both - first, scale


def packed_kernel(
    chunks, hidden, grad, out, flag_out,
    held_hidden, rows32, ht, gbuf, qsend, qrecv, own, sa, sb,
    xas, y1as, y2as, y1bs, y2bs, xbs, xa, y1a, y2a, y1b, y2b, xb, ns, nr, held, hs, hr, direct, flag, fsend, frecv,
    hsem, gsem, core_s, core_r, x_s, x_r, y1_s, y1_r, y2_s, y2_r, node_s, node_r, half_s, half_r, direct_s, direct_r, flag_s, flag_r,
):
    me = lax.axis_index("node")
    loc = lax.axis_index("local")
    c, x, y = lax.rem(loc, NC), lax.rem(lax.div(loc, NC), NX), lax.div(loc, NC * NX)
    far, sides = lax.rem(y + 2, NY), (lax.rem(y + 1, NY), lax.rem(y + 3, NY))
    other = 1 - x
    x_hi, z = lax.div(me, NZ), lax.rem(me, NZ)
    relayed = chunks // 4
    opposite = {"node": me + NZ * (1 - 2 * x_hi)}

    def at_y(row):
        return {"local": (row * NX + x) * NC + c}

    sibling = {"local": loc + 1 - 2 * c}
    across = {"local": loc + NC * (1 - 2 * x)}
    ring = [at_y(row) for row in sides]
    mates = [
        {"local": (lax.rem(y + j // 4, NY) * NX + lax.rem(x + j // 2 % 2, NX)) * NC + lax.rem(c + j % 2, NC)}
        for j in range(1, NY * NX * NC)
    ]
    nodes = [{"node": lax.rem(x_hi + j // NZ, NX_HI) * NZ + lax.rem(z + j % NZ, NZ)} for j in range(1, N_NODE)]

    def remote(src, dst, s, r, device):
        return pltpu.make_async_remote_copy(
            src_ref=src, dst_ref=dst, send_sem=s, recv_sem=r, device_id=device, device_id_type=MESH
        )

    def load(t):
        cols = pl.ds(pl.multiple_of(t * SPAN, SPAN), SPAN)
        return pltpu.make_async_copy(grad.at[:, cols], gbuf.at[lax.rem(t, 3)], gsem.at[lax.rem(t, 3)])

    def turn(t):
        odd = lax.rem(t, 2)
        return lax.rem(y + 1 + 2 * odd, NY), lax.rem(y + 3 - 2 * odd, NY)

    def pack(first, second, scale):
        both = first + second
        excess = jnp.maximum(jnp.abs(both), jnp.abs(second) * 4096.0) - scale
        width = scale.shape[-1]
        flag[:, :width] = jnp.maximum(flag[:, :width], jnp.max(excess.reshape(-1, 8, width), axis=0))
        return both + jnp.where(both < 0.0, -scale, scale)

    def join(left, right):
        return left[0] + right[0], left[1] + right[1], jnp.minimum(left[2], right[2])

    def rows_of(index, count):
        return pl.ds(pl.multiple_of(index * count, 8), count)

    barrier = pltpu.get_barrier_semaphore()
    peers = mates + nodes
    bring = pltpu.make_async_copy(hidden, held_hidden, hsem)
    bring.start()
    load(0).start()
    load(1).start()
    for peer in peers:
        pl.semaphore_signal(barrier, inc=1, device_id=peer, device_id_type=MESH)
    flag[...] = jnp.full((8, WORDS), -1.0, F32)
    bring.wait()
    for n in range(N_NODE):
        turned = held_hidden[:, n * 128 : (n + 1) * 128].astype(F32).T
        for block in range(NY * NX * NC):
            yo, xo, co = block // (NX * NC), block // NC % NX, block % NC
            if n < NODE_A:
                to = (xo * NY + yo) * ROWS_A + n * 8
            else:
                to = SEC_A + (yo * NX + xo) * ROWS_B + (n - NODE_A) * 8
            rows32[co * HALF + to : co * HALF + to + 8] = turned[block * 8 : block * 8 + 8]
    ht[...] = rows32[...].astype(BF16)

    def core_copy(t):
        k = lax.rem(t, SLOTS)
        return remote(qsend.at[lax.rem(t, 2)], qrecv.at[t], core_s.at[k], core_r.at[k], sibling)

    def xa_copy(t):
        k = lax.rem(t, SLOTS)
        return remote(xas.at[k], xa.at[t], x_s.at[k, 0], x_r.at[k, 0], across)

    def xb_copy(t):
        k = lax.rem(t, SLOTS)
        return remote(xbs.at[k], xb.at[t], x_s.at[k, 1], x_r.at[k, 1], across)

    def y1a_copy(t):
        k = lax.rem(t, SLOTS)
        return remote(y1as.at[k], y1a.at[t], y1_s.at[k, 2], y1_r.at[k, 2], at_y(turn(t)[0]))

    def y1b_copy(t, d):
        k = lax.rem(t, SLOTS)
        return remote(y1bs.at[k, d], y1b.at[t, d], y1_s.at[k, d], y1_r.at[k, d], ring[d])

    def y2a_copy(t, late):
        k = lax.rem(t, SLOTS)
        return remote(
            y2as.at[k, late], y2a.at[t, late], y2_s.at[k, 2, late], y2_r.at[k, 2, late], at_y(turn(t)[1 - late])
        )

    def y2b_copy(t, d, late):
        k = lax.rem(t, SLOTS)
        return remote(
            y2bs.at[k, d, late], y2b.at[t, d, late], y2_s.at[k, d, late], y2_r.at[k, d, late], ring[d]
        )

    def z_copies(group):
        k = lax.rem(group, SLOTS)
        return [
            remote(
                ns.at[k, lax.rem(z + j, NZ)], nr.at[group, z],
                node_s.at[k], node_r.at[k], {"node": x_hi * NZ + lax.rem(z + j, NZ)},
            )
            for j in range(1, NZ)
        ]

    def z_all(group):
        k, count = lax.rem(group, SLOTS), pl.ds(0, NZ - 1)
        return remote(
            ns.at[k, count], nr.at[group, count],
            node_s.at[k], node_r.at[k], opposite,
        )

    def direct_copies(group):
        k, g = lax.rem(group, SLOTS), group - relayed
        return [
            remote(
                ns.at[k, lax.rem(z + j % NZ, NZ), lax.rem(x_hi + j // NZ, NX_HI)], direct.at[g, j],
                direct_s.at[g], direct_r.at[g],
                {"node": lax.rem(x_hi + j // NZ, NX_HI) * NZ + lax.rem(z + j % NZ, NZ)},
            )
            for j in range(1, N_NODE)
        ]

    def half_copy(group):
        k = lax.rem(group, SLOTS)
        return remote(hs.at[k], hr.at[group], half_s.at[k], half_r.at[k], opposite)

    def compute(t, mine):
        for first in range(0, HALF, 128):
            start = (c if mine else 1 - c) * HALF + first
            rows = pl.ds(pl.multiple_of(start, 128), 128)
            part = jnp.dot(ht[rows, :], gbuf[lax.rem(t, 3)], preferred_element_type=F32)
            for j in range(WORDS // QB):
                one, power_one = block_levels(part[:, 2 * j * QB : (2 * j + 1) * QB])
                two, power_two = block_levels(part[:, (2 * j + 1) * QB : (2 * j + 2) * QB])
                one, two = one * (power_one * 64.0), two * (power_two * (1.0 / 64.0))
                least = jnp.minimum(power_one, power_two)
                scale = jnp.broadcast_to(least * 2.0**17, (128, QB))
                at = slice(first, first + 128), slice(j * QB, (j + 1) * QB)
                if mine:
                    for i, value in enumerate((one, two, scale)):
                        own[lax.rem(t, 2), i, *at] = value
                else:
                    excess = jnp.maximum(power_one, power_two) - least * 32.0
                    flag[:, :QB] = jnp.maximum(flag[:, :QB], jnp.max(excess.reshape(-1, 8, 1), axis=0))
                    both = one + two
                    qsend[lax.rem(t, 2), *at] = both + jnp.where(both < 0.0, -scale, scale)

    def compute_theirs(t):
        pl.when(t + 2 < chunks)(lambda: load(t + 2).start())
        load(t).wait()
        compute(t, False)

        @pl.when(t == 0)
        def _():
            pl.semaphore_wait(barrier, len(peers))

        core_copy(t).start()

    def compute_mine(t):
        compute(t, True)

    def stage1(t):
        k = lax.rem(t, SLOTS)
        core_copy(t).wait()

        def pair(first, index, count):
            rows = pl.ds(pl.multiple_of(first + index * count, 8), count)
            return join(unpack(qrecv[t, rows]), tuple(own[lax.rem(t, 2), i, rows] for i in range(3)))

        for d in range(2):
            y1bs[k, d] = pack(*pair(SEC_A, far * NX + d, ROWS_B))
            y1b_copy(t, d).start()
        xas[k] = pack(*pair(0, other, NY * ROWS_A))
        xa_copy(t).start()
        for d in range(2):
            y2bs[k, d, 0] = pack(*pair(SEC_A, sides[d] * NX + 1 - d, ROWS_B))
            y2b_copy(t, d, 0).start()
        for i, value in enumerate(pair(0, x, NY * ROWS_A)):
            sa[k, i] = value
        for j, index in enumerate((sides[0] * NX, sides[1] * NX + 1, y * NX, y * NX + 1)):
            for i, value in enumerate(pair(SEC_A, index, ROWS_B)):
                sb[k, j, i] = value

    def stage2(t):
        k = lax.rem(t, SLOTS)
        for d in range(2):
            y1b_copy(t, d).wait()
            y2bs[k, d, 1] = pack(*join(unpack(y1b[t, d]), tuple(sb[k, d, i] for i in range(3))))
            y2b_copy(t, d, 1).start()
        xa_copy(t).wait()

        def pair(row):
            rows = rows_of(row, ROWS_A)
            return join(unpack(xa[t, rows]), tuple(sa[k, i, rows] for i in range(3)))

        ahead, behind = turn(t)
        y1as[k] = pack(*pair(far))
        y1a_copy(t).start()
        y2as[k, 0] = pack(*pair(behind))
        y2a_copy(t, 0).start()
        for row in (ahead, y):
            for i, value in enumerate(pair(row)):
                sa[k, i, rows_of(row, ROWS_A)] = value

    def stage3(t):
        k = lax.rem(t, SLOTS)
        y1a_copy(t).wait()
        rows = rows_of(turn(t)[0], ROWS_A)
        y2as[k, 1] = pack(*join(unpack(y1a[t]), tuple(sa[k, i, rows] for i in range(3))))
        y2a_copy(t, 1).start()
        for d in range(2):
            for late in range(2):
                y2b_copy(t, d, late).wait()

        def pair(index):
            mine = tuple(sb[k, 2 + index, i] for i in range(3))
            return join(join(unpack(y2b[t, 0, 1 - index]), unpack(y2b[t, 1, index])), mine)

        xbs[k] = pack(*pair(other))
        xb_copy(t).start()
        for i, value in enumerate(pair(x)[:2]):
            sb[k, 0, i] = value

    def stage4(t):
        k = lax.rem(t, SLOTS)
        y2a_copy(t, 0).wait()
        y2a_copy(t, 1).wait()
        rows = rows_of(y, ROWS_A)
        left, right = unpack(y2a[t, 0]), unpack(y2a[t, 1])
        sum_a = [sa[k, i, rows] + left[i] + right[i] for i in range(2)]
        xb_copy(t).wait()
        last = unpack(xb[t])
        sum_b = [sb[k, 0, i] + last[i] for i in range(2)]
        group = lax.rem(lax.div(t, 2), SLOTS)
        for j in range(WORDS // QB):
            cut = slice(j * QB, (j + 1) * QB)
            for total, node, count in ((sum_a, 0, NODE_A), (sum_b, NODE_A, NODE_B)):
                pieces = [
                    quantize(total[0][:, cut] * (1.0 / 4096.0)).reshape(count, 8, QB),
                    quantize(total[1][:, cut]).reshape(count, 8, QB),
                ]
                blocks = jnp.concatenate(pieces, axis=1).astype(BF16)
                for n in range(count):
                    ns[group, (node + n) % NZ, (node + n) // NZ, lax.rem(t, 2), :, cut] = blocks[n]

        @pl.when((lax.rem(t, 2) == 1) & (t < 2 * relayed))
        def _():
            for copy in z_copies(lax.div(t, 2)):
                copy.start()

        @pl.when((lax.rem(t, 2) == 1) & (t >= 2 * relayed))
        def _():
            for copy in direct_copies(lax.div(t, 2)):
                copy.start()

    def stage5(t):
        group = lax.div(t, 2)
        k = lax.rem(group, SLOTS)
        z_all(group).wait()

        def total(index):
            value = ns[k, z, index, :].astype(F32)
            for j in range(1, NZ):
                value = value + nr[group, lax.rem(z + j, NZ), index, :].astype(F32)
            return value

        hs[k, :] = total(1 - x_hi)
        half_copy(group).start()
        held[k, :] = total(x_hi)

    def stage6(t):
        group = lax.div(t, 2)
        k = lax.rem(group, SLOTS)
        half_copy(group).wait()
        for part in range(2):
            store(t - 1 + part, held[k, part] + hr[group, part])

    def store(t, total):
        for j in range(SPAN // QB):
            cols = pl.ds(pl.multiple_of(t * SPAN + j * QB, QB), QB)
            row, lane = 8 * (j % 2), j // 2 * QB
            out[:, cols] = total[row : row + 8, lane : lane + QB]

    def finish(group):
        g, count = group - relayed, pl.ds(1, N_NODE - 1)
        remote(direct.at[g, count], direct.at[g, count], direct_s.at[g], direct_r.at[g], opposite).wait()
        total = ns[group % SLOTS, z, x_hi].astype(F32)
        for j in range(1, N_NODE):
            total = total + direct[g, j].astype(F32)
        for part in range(2):
            store(2 * group + part, total[part])

    rounds = (mates, nodes)
    places = (0, len(mates))

    def flag_copies(index):
        return [
            remote(
                fsend.at[index], frecv.at[places[index] + i],
                flag_s.at[places[index] + i], flag_r.at[places[index] + i], device,
            )
            for i, device in enumerate(rounds[index])
        ]

    def flag_round(index):
        if index == 0:
            value = functools.reduce(jnp.maximum, [flag[:, j * QB : (j + 1) * QB] for j in range(WORDS // QB)])
        else:
            value = fsend[index - 1]
            for i, copy in enumerate(flag_copies(index - 1)):
                copy.wait()
                value = jnp.maximum(value, frecv[places[index - 1] + i])
        if index == len(rounds):
            flag_out[0, 0] = jnp.max(value)
            return
        fsend[index] = value
        for copy in flag_copies(index):
            copy.start()

    def step(t, carry):
        def run(body, stage, end=chunks, odd=False):
            now = t - PACKED_LAG[stage]
            inside = (now >= 0) & (now < end)
            if odd:
                inside = inside & (lax.rem(t, 2) == (PACKED_LAG[stage] + 1) % 2)
            pl.when(inside)(lambda: body(now))

        run(compute_theirs, 0)
        pl.when((t >= 2) & (t <= chunks))(lambda: stage1(t - 1))
        run(stage3, 3)
        pl.when(t == chunks - 1 + PACKED_LAG[3])(lambda: flag_round(0))
        run(compute_mine, 0)
        pl.when(t == 0)(lambda: stage1(t))
        run(stage2, 2)
        run(stage4, 4)
        pl.when(t == chunks - 1 + PACKED_LAG[4])(lambda: flag_round(1))
        run(stage5, 5, 2 * relayed, True)
        run(stage6, 6, 2 * relayed, True)
        return carry

    lax.fori_loop(0, chunks + PACKED_LAG[4], step, 0)
    for group in range(relayed, chunks // 2):
        finish(group)
    flag_round(2)


def arrange(hidden_acts):
    tokens = hidden_acts.shape[0]
    blocked = hidden_acts.T.reshape(N_NODE, NY, NX, NC, 8, tokens)
    first = blocked[:NODE_A].transpose(3, 2, 1, 0, 4, 5).reshape(NC, SEC_A, tokens)
    second = blocked[NODE_A:].transpose(3, 1, 2, 0, 4, 5).reshape(NC, SEC_B, tokens)
    return jnp.concatenate([first, second], axis=1).reshape(NC * HALF, tokens)


def call(body, chunks, collective_id, hidden, grad_out, has_flag, scratch):
    tokens, width = grad_out.shape
    vmem_spec = pl.BlockSpec(memory_space=pltpu.VMEM)
    out_shape, out_specs = [jax.ShapeDtypeStruct((8, width), F32)], [vmem_spec]
    if has_flag:
        out_shape.append(jax.ShapeDtypeStruct((1, 1), F32))
        out_specs.append(pl.BlockSpec(memory_space=pltpu.SMEM))
    return pl.pallas_call(
        functools.partial(body, chunks),
        out_shape=out_shape,
        in_specs=[pl.BlockSpec(memory_space=pl.ANY) if has_flag else vmem_spec, pl.BlockSpec(memory_space=pl.ANY)],
        out_specs=out_specs,
        scratch_shapes=scratch,
        compiler_params=pltpu.CompilerParams(
            collective_id=collective_id, has_side_effects=True, vmem_limit_bytes=58 * 2**20
        ),
        cost_estimate=pl.CostEstimate(
            flops=2 * tokens * NC * HALF * width, bytes_accessed=2 * tokens * (width + NC * HALF), transcendentals=0
        ),
    )(hidden, grad_out)


def wide(ht, grad_out):
    tokens, width = grad_out.shape
    chunks, half = width // COLS, COLS // 2
    vmem, dma = pltpu.VMEM, pltpu.SemaphoreType.DMA
    scratch = [
        vmem((3, tokens, COLS), BF16),
        vmem((4, HALF, COLS), BF16),
        vmem((chunks, HALF, COLS), BF16),
        vmem((chunks, NX, NY, ROWS_A, COLS), F32),
        vmem((chunks, NY, NX, ROWS_B, COLS), F32),
        vmem((chunks, NY, ROWS_A, COLS), F32),
        vmem((chunks, 2, ROWS_A, half), F32),
        vmem((chunks, 2, ROWS_A, COLS), F32),
        vmem((chunks, 2, NX, ROWS_B, half), F32),
        vmem((chunks, 2, NX, ROWS_B, COLS), F32),
        vmem((chunks, ROWS_B, COLS), F32),
        vmem((chunks, N_NODE, 16, half), BF16),
        vmem((chunks, N_NODE, 16, half), BF16),
        dma((3,)),
        *[dma((SLOTS,))] * 2,
        *[dma((SLOTS, 2))] * 2,
        *[dma((SLOTS, 2, 2))] * 4,
        *[dma((SLOTS, N_NODE))] * 2,
    ]
    return call(wide_kernel, chunks, 1, ht, grad_out, False, scratch)[0]


def packed(hidden_acts, grad_out):
    tokens, width = grad_out.shape
    chunks = width // SPAN
    vmem, dma = pltpu.VMEM, pltpu.SemaphoreType.DMA
    sizes = [(NY * ROWS_A,), (ROWS_A,), (2, ROWS_A), (2, ROWS_B), (2, 2, ROWS_B), (ROWS_B,)]
    scratch = [
        vmem((tokens, NC * HALF), BF16),
        vmem((NC * HALF, tokens), F32),
        vmem((NC * HALF, tokens), BF16),
        vmem((3, tokens, SPAN), BF16),
        vmem((2, HALF, WORDS), F32),
        vmem((chunks, HALF, WORDS), F32),
        vmem((2, 3, HALF, WORDS), F32),
        vmem((SLOTS, 3, NY * ROWS_A, WORDS), F32),
        vmem((SLOTS, 4, 3, ROWS_B, WORDS), F32),
        *[vmem((SLOTS, *size, WORDS), F32) for size in sizes],
        *[vmem((chunks, *size, WORDS), F32) for size in sizes],
        vmem((SLOTS, NZ, NX_HI, 2, 16, WORDS), BF16),
        vmem((chunks // 2, NZ, NX_HI, 2, 16, WORDS), BF16),
        vmem((SLOTS, 2, 16, WORDS), F32),
        vmem((SLOTS, 2, 16, WORDS), F32),
        vmem((chunks // 2, 2, 16, WORDS), F32),
        vmem((chunks // 2 - chunks // 4, N_NODE, 2, 16, WORDS), BF16),
        vmem((8, WORDS), F32),
        vmem((2, 8, QB), F32),
        vmem((22, 8, QB), F32),
        pltpu.SemaphoreType.DMA,
        dma((3,)),
        *[dma((SLOTS,))] * 2,
        *[dma((SLOTS, 2))] * 2,
        *[dma((SLOTS, 3))] * 2,
        *[dma((SLOTS, 3, 2))] * 2,
        *[dma((SLOTS,))] * 4,
        *[dma((chunks // 2 - chunks // 4,))] * 2,
        *[dma((22,))] * 2,
    ]
    out, flag = call(packed_kernel, chunks, 0, hidden_acts, grad_out, True, scratch)
    return out, flag[0, 0] >= 0.0


def per_device(hidden_acts, grad_out):
    out, misfit = packed(hidden_acts, grad_out)
    return lax.cond(misfit, lambda: wide(arrange(hidden_acts), grad_out), lambda: out)


def solution(mesh):
    return jax.shard_map(
        per_device,
        mesh=mesh,
        in_specs=(P(("node", "local"), None), P(("node", "local"), None)),
        out_specs=P(("node", "local"), None),
        check_vma=False,
    )
```
